32 devices in a mesh: groups: 2 (over x), blk: 8 (over z, y), mand: 2 (over core).
Axes of the slice: x: 2, y: 2, z: 4, core: 2. Of those that a mesh axis runs over, the one named last changes fastest.
Arguments:
- holdings: float32 [256, 8192], P(('groups', 'mand'), 'blk'), parts along dimension 0, may hold values from -6 to 6
- eligible: int32 [256, 8192], P(('groups', 'mand'), 'blk'), parts along dimension 0, may hold values 0 or 1
- returns_mu: float32 [16384], P(('groups', 'blk')), parts along dimension 0, may hold values from -6 to 6
- cov_diag: bfloat16 [64, 256, 256], P(('groups', 'blk')), parts along dimension 0, as said below
- cov_pairs: bfloat16 [1024, 256, 256], P(('groups', 'blk')), parts along dimension 0, may hold values from -0.0625 to 0.0625
- pair_slots: int32 [16, 64, 2], P(('groups', 'blk')), parts along dimension 0, may hold values from 0 to 15, as said below
- need_table: int32 [16, 8, 2], P('groups'), parts along dimension 0, may hold values from -1 to 3, as said below
- break_index: int32 [64], P(('groups', 'blk')), parts along dimension 0, may hold values from 0 to 7
- break_levels: float32 [8], replicated, may hold values from 0.1 to 1
- cost_slopes: float32 [2, 128], P(None, 'mand'), may hold values from 0.05 to 0.5
Outputs:
- traded: float32 [256, 8192], P(('groups', 'mand'), 'blk'), parts along dimension 0
- dual: float32 [256, 8192], P(('groups', 'mand'), 'blk'), parts along dimension 0
The draws below stay inside these ranges and needn't reach their ends.
There are 2 independent parts, one for each index of `groups`. The reference program is written for one: setup_inputs(seed, part) draws one part's arguments, and reference() takes and returns one part's arrays. A program takes and returns all parts, laid end to end along the dimension named above; an argument that names none is the same for every part. Nothing has to cross between parts.
Inputs may be any that keep to these rules, and one draw needn't show every extreme that they name: need_table[o, r, :] holds distinct local block indices of device r that device o needs, then -1 for the rest; every device needs all 2 slots from itself; some device needs 2 blocks from every device. `pair_slots`: each pair's two slot numbers differ and name non-empty entries of its device's need_table row; every non-empty entry is named by some pair of that device. `cov_diag`: each block is symmetric.
All inputs are finite; a program needn't handle non-finite values. No bound on the sum of `eligible` on one device may be relied on, other than what follows from the above.
Results may differ from the reference program's by a relative error of at most 0.0029.
Values may be sent and summed in bfloat16 or wider, within the bound.
No kernel may reach another device: no remote copies, remote signals or barrier semaphores. Data moves between devices by JAX's collectives and lax.ppermute only.
A program may use at most 128 MiB of HBM per device.

```python
import math
import jax
import jax.numpy as jnp
from jax import lax

BS = 256
MAND = 128
BLK_DEV = 4
P_DEV = 64
CAP = 2
LEVELS = 8
ITERS = 2
NBLOCKS = 32
ASSETS = 8192
PAIRS = 512
N_BLK = 8


def pair_layout(key):
    key_counts, key_full, key_pick, key_order = jax.random.split(key, 4)
    owner_ids = jnp.arange(N_BLK, dtype=jnp.int32)
    counts = jax.random.randint(key_counts, (N_BLK, N_BLK), 0, CAP + 1).astype(jnp.int32)
    full_owner = jax.random.randint(key_full, (), 0, N_BLK).astype(jnp.int32)
    forced = (owner_ids[:, None] == full_owner) | (owner_ids[:, None] == owner_ids[None, :])
    counts = jnp.where(forced, CAP, counts)
    scores = jax.random.randint(key_pick, (N_BLK, N_BLK, BLK_DEV), 0, 1 << 20).astype(jnp.int32) * BLK_DEV + jnp.arange(BLK_DEV, dtype=jnp.int32)
    ranked = jnp.argsort(scores, axis=2)[:, :, :CAP].astype(jnp.int32)
    columns = jnp.arange(CAP, dtype=jnp.int32)
    need_table = jnp.where(columns[None, None, :] < counts[:, :, None], ranked, -1).astype(jnp.int32)
    slot_total = N_BLK * CAP
    live = need_table.reshape(N_BLK, slot_total) >= 0
    slot_ids = jnp.arange(slot_total, dtype=jnp.int32)
    order_keys = jax.random.randint(key_order, (N_BLK, slot_total), 0, 1 << 20).astype(jnp.int32) * slot_total + slot_ids
    order_keys = jnp.where(live, order_keys, order_keys + (1 << 20) * slot_total)
    ordering = jnp.argsort(order_keys, axis=1).astype(jnp.int32)
    live_count = jnp.sum(live.astype(jnp.int32), axis=1)
    positions = jnp.arange(2 * P_DEV, dtype=jnp.int32)[None, :] % live_count[:, None]
    chosen = jnp.take_along_axis(ordering, positions, axis=1)
    return (need_table, chosen.reshape(N_BLK, P_DEV, 2).astype(jnp.int32))


def draw_need_table(key, part):
    need_table, pair_slots = pair_layout(key)
    return need_table


def draw_pair_slots(key, part):
    need_table, pair_slots = pair_layout(key)
    return pair_slots


def draw_cov_diag(key, part):
    key = jax.random.fold_in(key, 5)
    key_noise, key_scale = jax.random.split(key)
    nblocks = BLK_DEV * N_BLK
    gaussian = jax.random.normal(key_noise, (nblocks, BS, BS), jnp.float32)
    symmetric = (gaussian + jnp.swapaxes(gaussian, 1, 2)) * (0.35 / math.sqrt(2.0 * BS))
    scales = jnp.exp(jax.random.uniform(key_scale, (nblocks, BS), jnp.float32, math.log(0.5), math.log(2.0)))
    identity = jnp.eye(BS, dtype=jnp.float32)
    return (symmetric + identity[None, :, :] * scales[:, :, None]).astype(jnp.bfloat16)


def plant(values, own_key, least, high):
    place = [jax.random.randint(jax.random.fold_in(own_key, axis), (), 0, length) for axis, length in enumerate(values.shape)]
    main_axis = values.shape.index(max(values.shape))
    next_to = place[:main_axis] + [(place[main_axis] + 1) % values.shape[main_axis]] + place[main_axis + 1:]
    return values.at[tuple(place)].set(least).at[tuple(next_to)].set(high)


def levels(stream_key, dims, shards, smallest, largest):
    def one(position, shards_of):
        steps = jax.random.uniform(jax.random.fold_in(jax.random.fold_in(stream_key, 6), position), (shards_of,), jnp.float32, smallest / len(shards), largest / len(shards))
        return jnp.repeat(jnp.exp(steps), dims[position] // shards_of).reshape((-1,) + (1,) * (len(dims) - position - 1))

    gain = one(*shards[0])
    for cut in shards[1:]:
        gain = gain * one(*cut)
    return gain


def noise(stream_key, shape, spread, reach, shards=(), kind=jnp.bfloat16):
    array = spread * jax.random.normal(stream_key, shape, jnp.float32)
    if shards:
        array = array * levels(stream_key, shape, shards, -0.22, 0.18)
    return jnp.clip(array, -reach, reach).astype(kind)


def setup_inputs(seed: int = 0, part: int = 0) -> dict:
    splits = jax.random.split(jax.random.key(seed), 11)
    part_keys = jax.random.split(jax.random.fold_in(splits[10], part), 11)
    holdings = noise(part_keys[0], (MAND, ASSETS), 1.0, 6.0, ((0, 2), (1, 8)), jnp.float32)
    eligible = plant((jax.random.randint(part_keys[1], (MAND, ASSETS), 0, 4) < 3).astype(jnp.int32), jax.random.fold_in(part_keys[1], 1), 0, 1)
    returns_mu = noise(part_keys[2], (ASSETS,), 1.0, 6.0, ((0, 8),), jnp.float32)
    cov_diag = draw_cov_diag(jax.random.fold_in(jax.random.fold_in(splits[10], part), 71), part)
    cov_pairs = noise(part_keys[4], (PAIRS, BS, BS), (BS * 2 * P_DEV // BLK_DEV) ** -0.5, 0.0625, ((0, 8),))
    pair_slots = draw_pair_slots(jax.random.fold_in(jax.random.fold_in(splits[10], part), 71), part)
    need_table = draw_need_table(jax.random.fold_in(jax.random.fold_in(splits[10], part), 71), part)
    break_index = plant(jax.random.randint(part_keys[7], (NBLOCKS,), 0, LEVELS), jax.random.fold_in(part_keys[7], 1), 0, LEVELS - 1).astype(jnp.int32)
    break_levels = jnp.clip(jnp.exp(jax.random.uniform(splits[8], (LEVELS,), jnp.float32, math.log(0.1), math.log(1.0))), 0.1, 1.0)
    cost_slopes = jnp.clip(jnp.exp(math.log(0.5) - 2.3025851 * jax.random.uniform(splits[9], (2, MAND), jnp.float32) ** levels(splits[9], (2, MAND), ((1, 2),), -0.2, 0.2)), 0.05, 0.5)
    return {"holdings": holdings, "eligible": eligible, "returns_mu": returns_mu, "cov_diag": cov_diag, "cov_pairs": cov_pairs, "pair_slots": pair_slots, "need_table": need_table, "break_index": break_index, "break_levels": break_levels, "cost_slopes": cost_slopes}


STEP_SIZE = 0.5
RISK_AVERSION = 1.0
PENALTY = 1.0


def level_lookup(break_index, break_levels):
    matches = break_index[:, None] == jnp.arange(LEVELS, dtype=jnp.int32)[None, :]
    return jnp.sum(jnp.where(matches, break_levels[None, :], jnp.float32(0.0)), axis=1)


def trade_prox(values, slope_low, slope_high, cost_knee):
    magnitude = jnp.abs(values)
    lower_part = jnp.minimum(jnp.maximum(magnitude - slope_low, 0.0), cost_knee)
    upper_part = jnp.maximum(magnitude - slope_high - cost_knee, 0.0)
    return jnp.sign(values) * (lower_part + upper_part)


def reference(holdings, eligible, returns_mu, cov_diag, cov_pairs, pair_slots, need_table, break_index, break_levels, cost_slopes):
    nblocks = BLK_DEV * N_BLK

    def to_blocks(values):
        return values.reshape(MAND, nblocks, BS).transpose(1, 0, 2)

    initial = to_blocks(holdings)
    allowed = to_blocks(eligible).astype(jnp.float32)
    expected = returns_mu.reshape(nblocks, 1, BS)
    cost_knee = level_lookup(break_index, break_levels)[:, None, None]
    slope_low = (cost_slopes[0] / PENALTY)[None, :, None]
    slope_high = ((cost_slopes[0] + cost_slopes[1]) / PENALTY)[None, :, None]
    diag_blocks = cov_diag.astype(jnp.float32)
    owner_cov = cov_pairs.reshape(N_BLK, P_DEV, BS, BS)
    sources = jnp.arange(N_BLK * CAP, dtype=jnp.int32) // CAP
    primal = initial
    traded = initial
    dual = jnp.zeros_like(initial)
    for iteration in range(ITERS):
        x_wire = primal.astype(jnp.bfloat16).astype(jnp.float32)
        risk_grad = jnp.einsum("bmj,bjk->bmk", x_wire, diag_blocks, precision=lax.Precision.HIGHEST)

        def owner_step(running, inputs):
            owner_need, owner_pairs, owner_blocks = inputs
            local_ids = owner_need.reshape(-1).astype(jnp.int32)
            global_ids = sources * BLK_DEV + jnp.maximum(local_ids, 0)
            first_ids = global_ids[owner_pairs[:, 0]]
            second_ids = global_ids[owner_pairs[:, 1]]
            cov_blocks = owner_blocks.astype(jnp.float32)
            to_first = jnp.einsum("pmk,pjk->pmj", x_wire[second_ids], cov_blocks, precision=lax.Precision.HIGHEST)
            to_second = jnp.einsum("pmj,pjk->pmk", x_wire[first_ids], cov_blocks, precision=lax.Precision.HIGHEST)
            running = running.at[first_ids].add(to_first).at[second_ids].add(to_second)
            return running, None

        pair_terms, unused_out = lax.scan(owner_step, jnp.zeros_like(primal), (need_table, pair_slots, owner_cov))
        grad = risk_grad + pair_terms
        primal = allowed * (primal - STEP_SIZE * (RISK_AVERSION * grad - expected + PENALTY * (primal - traded + dual)))
        shifted = primal + dual - initial
        traded = initial + trade_prox(shifted, slope_low, slope_high, cost_knee)
        dual = dual + primal - traded
    traded_out = traded.transpose(1, 0, 2).reshape(MAND, nblocks * BS)
    dual_out = dual.transpose(1, 0, 2).reshape(MAND, nblocks * BS)
    return traded_out, dual_out
```

```python
import functools

import jax
import jax.numpy as jnp
from jax import lax
from jax.experimental import pallas as pl
from jax.experimental.pallas import tpu as pltpu
from jax.sharding import PartitionSpec as P

ITERS = 2
STEP_SIZE = 0.5
RISK_AVERSION = 1.0
PENALTY = 1.0
CHUNKS = 8

VMEM = pl.BlockSpec(memory_space=pltpu.VMEM)
SMEM = pl.BlockSpec(memory_space=pltpu.SMEM)
ANY = pl.BlockSpec(memory_space=pl.ANY)
PARAMS = pltpu.CompilerParams(vmem_limit_bytes=48 * 1024 * 1024)


def fill_outgoing(served_ref, wire_ref, outgoing_ref):
    def one(slot, carry):
        outgoing_ref[slot] = wire_ref[jnp.maximum(served_ref[slot], 0)]
        return carry

    lax.fori_loop(0, outgoing_ref.shape[0], one, 0, unroll=4)


def pack_kernel(served_ref, holdings_ref, outgoing_ref, wire_ref):
    size = wire_ref.shape[2]
    for block in range(wire_ref.shape[0]):
        wire_ref[block] = holdings_ref[:, block * size : (block + 1) * size].astype(jnp.bfloat16)
    fill_outgoing(served_ref, wire_ref, outgoing_ref)


def pairs_kernel(pairs_ref, rows_ref, cov_ref, partial_ref, cov_vmem, total, sems):
    pairs = cov_ref.shape[0]
    step = pairs // CHUNKS
    copies = [
        pltpu.make_async_copy(
            cov_ref.at[pl.ds(chunk * step, step)],
            cov_vmem.at[pl.ds(chunk * step, step)],
            sems.at[chunk],
        )
        for chunk in range(CHUNKS)
    ]
    for copy in copies:
        copy.start()
    total[...] = jnp.zeros_like(total)
    for chunk, copy in enumerate(copies):
        copy.wait()

        def one(pair, carry):
            first = pairs_ref[0, pair, 0]
            second = pairs_ref[0, pair, 1]
            block = cov_vmem[pair]
            to_first = lax.dot_general(
                rows_ref[second], block, (((1,), (1,)), ((), ())), preferred_element_type=jnp.float32
            )
            to_second = jnp.dot(rows_ref[first], block, preferred_element_type=jnp.float32)
            total[first] += to_first
            total[second] += to_second
            return carry

        lax.fori_loop(chunk * step, (chunk + 1) * step, one, 0, unroll=4)
    partial_ref[...] = total[...].astype(jnp.bfloat16)


def column(row, rows):
    square = (rows, rows)
    on_diagonal = lax.broadcasted_iota(jnp.int32, square, 0) == lax.broadcasted_iota(jnp.int32, square, 1)
    return jnp.sum(jnp.where(on_diagonal, row, 0.0), axis=1, keepdims=True)


def update_kernel(
    last,
    served_ref,
    knee_index_ref,
    knee_levels_ref,
    returned_ref,
    slopes_ref,
    holdings_ref,
    eligible_ref,
    expected_ref,
    diag_ref,
    *refs,
):
    if last:
        primal_ref, traded_ref, dual_ref, traded_out, dual_out, terms = refs
    else:
        primal_out, traded_out, dual_out, outgoing_ref, terms, wire_ref = refs
    blocks, rows, size = terms.shape
    terms[...] = jnp.zeros_like(terms)

    def one(slot, carry):
        local = served_ref[slot]

        @pl.when(local >= 0)
        def _():
            terms[local] += returned_ref[slot].astype(jnp.float32)

        return carry

    lax.fori_loop(0, returned_ref.shape[0], one, 0, unroll=4)
    low = column(slopes_ref[0:1, :] / PENALTY, rows)
    high = column((slopes_ref[0:1, :] + slopes_ref[1:2, :]) / PENALTY, rows)
    for block in range(blocks):
        span = pl.ds(block * size, size)
        initial = holdings_ref[:, span]
        primal = primal_ref[:, span] if last else initial
        x_wire = primal.astype(jnp.bfloat16)
        grad = jnp.dot(x_wire, diag_ref[block], preferred_element_type=jnp.float32) + terms[block]
        expected = expected_ref[:, span]
        allowed = eligible_ref[:, span].astype(jnp.float32)
        if last:
            dual = dual_ref[:, span]
            gap = primal - traded_ref[:, span] + dual
        else:
            dual = jnp.zeros_like(initial)
            gap = dual
        primal = allowed * (primal - STEP_SIZE * (RISK_AVERSION * grad - expected + PENALTY * gap))
        shifted = primal + dual - initial
        knee = knee_levels_ref[knee_index_ref[block]]
        magnitude = jnp.abs(shifted)
        moved = jnp.minimum(jnp.maximum(magnitude - low, 0.0), knee) + jnp.maximum(
            magnitude - high - knee, 0.0
        )
        traded = initial + jnp.where(shifted < 0.0, -moved, moved)
        traded_out[:, span] = traded
        dual_out[:, span] = dual + primal - traded
        if not last:
            primal_out[:, span] = primal
            wire_ref[block] = primal.astype(jnp.bfloat16)
    if not last:
        fill_outgoing(served_ref, wire_ref, outgoing_ref)


def body(
    holdings,
    eligible,
    returns_mu,
    cov_diag,
    cov_pairs,
    pair_slots,
    need_table,
    break_index,
    break_levels,
    cost_slopes,
):
    rows, assets = holdings.shape
    blocks, size, _ = cov_diag.shape
    owners = lax.axis_size("blk")
    my_index = lax.axis_index("blk")
    capacity = need_table.shape[2]
    slots = owners * capacity
    served = lax.dynamic_index_in_dim(need_table, my_index, 1, keepdims=False).reshape(-1)
    slot_shape = (slots, rows, size)
    wire_shape = pltpu.VMEM((blocks, rows, size), jnp.bfloat16)
    whole = jax.ShapeDtypeStruct((rows, assets), jnp.float32)
    outgoing_shape = jax.ShapeDtypeStruct(slot_shape, jnp.bfloat16)

    def exchange(values):
        sent = values.reshape(owners, capacity, rows, size)
        return lax.all_to_all(sent, "blk", split_axis=0, concat_axis=0, tiled=True).reshape(slot_shape)

    outgoing = pl.pallas_call(
        pack_kernel,
        out_shape=outgoing_shape,
        in_specs=[SMEM, VMEM],
        out_specs=VMEM,
        scratch_shapes=[wire_shape],
        compiler_params=PARAMS,
        name="pack_holdings",
    )(served, holdings)
    expected = returns_mu.reshape(1, assets)
    state = ()
    for iteration in range(ITERS):
        last = iteration == ITERS - 1
        slot_rows = exchange(outgoing)
        partial_sums = pl.pallas_call(
            pairs_kernel,
            out_shape=outgoing_shape,
            in_specs=[SMEM, VMEM, ANY],
            out_specs=VMEM,
            scratch_shapes=[
                pltpu.VMEM(cov_pairs.shape, jnp.bfloat16),
                pltpu.VMEM(slot_shape, jnp.float32),
                pltpu.SemaphoreType.DMA((CHUNKS,)),
            ],
            compiler_params=PARAMS,
            name="pair_products",
        )(pair_slots, slot_rows, cov_pairs)
        returned = exchange(partial_sums)
        outs = pl.pallas_call(
            functools.partial(update_kernel, last),
            out_shape=(whole, whole) if last else (whole, whole, whole, outgoing_shape),
            in_specs=[SMEM] * 3 + [VMEM] * (6 + len(state)),
            out_specs=(VMEM,) * (2 if last else 4),
            scratch_shapes=[pltpu.VMEM((blocks, rows, size), jnp.float32)] + ([] if last else [wire_shape]),
            compiler_params=PARAMS,
            name="update",
        )(
            served,
            break_index,
            break_levels,
            returned,
            cost_slopes,
            holdings,
            eligible,
            expected,
            cov_diag,
            *state,
        )
        if not last:
            *state, outgoing = outs
    return outs


def solution(mesh):
    placed = (
        P(("groups", "mand"), "blk"),
        P(("groups", "mand"), "blk"),
        P(("groups", "blk")),
        P(("groups", "blk"), None, None),
        P(("groups", "blk"), None, None),
        P(("groups", "blk"), None, None),
        P("groups", None, None),
        P(("groups", "blk")),
        P(),
        P(None, "mand"),
    )
    return jax.shard_map(
        body,
        mesh=mesh,
        in_specs=placed,
        out_specs=(P(("groups", "mand"), "blk"), P(("groups", "mand"), "blk")),
        check_vma=False,
    )
```

```python
import functools

import jax
import jax.numpy as jnp
from jax import lax
from jax.experimental import pallas as pl
from jax.experimental.pallas import tpu as pltpu
from jax.sharding import PartitionSpec as P

ITERS = 2
STEP_SIZE = 0.5
RISK_AVERSION = 1.0
PENALTY = 1.0

VMEM = pl.BlockSpec(memory_space=pltpu.VMEM)
SMEM = pl.BlockSpec(memory_space=pltpu.SMEM)
PARAMS = pltpu.CompilerParams(vmem_limit_bytes=24 * 1024 * 1024)


def fill_outgoing(served_ref, wire_ref, outgoing_ref):
    def one(slot, carry):
        outgoing_ref[slot] = wire_ref[jnp.maximum(served_ref[slot], 0)]
        return carry

    lax.fori_loop(0, outgoing_ref.shape[0], one, 0, unroll=4)


def pack_kernel(served_ref, holdings_ref, outgoing_ref, wire_ref):
    size = wire_ref.shape[2]
    for block in range(wire_ref.shape[0]):
        wire_ref[block] = holdings_ref[:, block * size : (block + 1) * size].astype(jnp.bfloat16)
    fill_outgoing(served_ref, wire_ref, outgoing_ref)


def pairs_kernel(pairs_ref, rows_ref, cov_ref, partial_ref, total):
    total[...] = jnp.zeros_like(total)

    def one(pair, carry):
        first = pairs_ref[0, pair, 0]
        second = pairs_ref[0, pair, 1]
        block = cov_ref[pair]
        to_first = lax.dot_general(
            rows_ref[second], block, (((1,), (1,)), ((), ())), preferred_element_type=jnp.float32
        )
        to_second = jnp.dot(rows_ref[first], block, preferred_element_type=jnp.float32)
        total[first] += to_first
        total[second] += to_second
        return carry

    lax.fori_loop(0, cov_ref.shape[0], one, 0, unroll=16)
    partial_ref[...] = total[...].astype(jnp.bfloat16)


def column(row, rows):
    square = (rows, rows)
    on_diagonal = lax.broadcasted_iota(jnp.int32, square, 0) == lax.broadcasted_iota(jnp.int32, square, 1)
    return jnp.sum(jnp.where(on_diagonal, row, 0.0), axis=1, keepdims=True)


def update_kernel(
    last,
    served_ref,
    knee_index_ref,
    knee_levels_ref,
    returned_ref,
    slopes_ref,
    holdings_ref,
    eligible_ref,
    expected_ref,
    diag_ref,
    *refs,
):
    if last:
        primal_ref, traded_ref, dual_ref, traded_out, dual_out, terms = refs
    else:
        primal_out, traded_out, dual_out, outgoing_ref, terms, wire_ref = refs
    blocks, rows, size = terms.shape
    terms[...] = jnp.zeros_like(terms)

    def one(slot, carry):
        local = served_ref[slot]

        @pl.when(local >= 0)
        def _():
            terms[local] += returned_ref[slot].astype(jnp.float32)

        return carry

    lax.fori_loop(0, returned_ref.shape[0], one, 0, unroll=4)
    low = column(slopes_ref[0:1, :] / PENALTY, rows)
    high = column((slopes_ref[0:1, :] + slopes_ref[1:2, :]) / PENALTY, rows)
    for block in range(blocks):
        span = pl.ds(block * size, size)
        initial = holdings_ref[:, span]
        primal = primal_ref[:, span] if last else initial
        x_wire = primal.astype(jnp.bfloat16)
        grad = jnp.dot(x_wire, diag_ref[block], preferred_element_type=jnp.float32) + terms[block]
        expected = expected_ref[:, span]
        allowed = eligible_ref[:, span].astype(jnp.float32)
        if last:
            dual = dual_ref[:, span]
            gap = primal - traded_ref[:, span] + dual
        else:
            dual = jnp.zeros_like(initial)
            gap = dual
        primal = allowed * (primal - STEP_SIZE * (RISK_AVERSION * grad - expected + PENALTY * gap))
        shifted = primal + dual - initial
        knee = knee_levels_ref[knee_index_ref[block]]
        magnitude = jnp.abs(shifted)
        moved = jnp.minimum(jnp.maximum(magnitude - low, 0.0), knee) + jnp.maximum(
            magnitude - high - knee, 0.0
        )
        traded = initial + jnp.where(shifted < 0.0, -moved, moved)
        traded_out[:, span] = traded
        dual_out[:, span] = dual + primal - traded
        if not last:
            primal_out[:, span] = primal
            wire_ref[block] = primal.astype(jnp.bfloat16)
    if not last:
        fill_outgoing(served_ref, wire_ref, outgoing_ref)


def body(
    holdings,
    eligible,
    returns_mu,
    cov_diag,
    cov_pairs,
    pair_slots,
    need_table,
    break_index,
    break_levels,
    cost_slopes,
):
    rows, assets = holdings.shape
    blocks, size, _ = cov_diag.shape
    owners = lax.axis_size("blk")
    my_index = lax.axis_index("blk")
    capacity = need_table.shape[2]
    slots = owners * capacity
    served = lax.dynamic_index_in_dim(need_table, my_index, 1, keepdims=False).reshape(-1)
    slot_shape = (slots, rows, size)
    wire_shape = pltpu.VMEM((blocks, rows, size), jnp.bfloat16)
    whole = jax.ShapeDtypeStruct((rows, assets), jnp.float32)
    outgoing_shape = jax.ShapeDtypeStruct(slot_shape, jnp.bfloat16)

    def exchange(values):
        sent = values.reshape(owners, capacity, rows, size)
        return lax.all_to_all(sent, "blk", split_axis=0, concat_axis=0, tiled=True).reshape(slot_shape)

    outgoing = pl.pallas_call(
        pack_kernel,
        out_shape=outgoing_shape,
        in_specs=[SMEM, VMEM],
        out_specs=VMEM,
        scratch_shapes=[wire_shape],
        compiler_params=PARAMS,
        name="pack_holdings",
    )(served, holdings)
    expected = returns_mu.reshape(1, assets)
    state = ()
    for iteration in range(ITERS):
        last = iteration == ITERS - 1
        slot_rows = exchange(outgoing)
        partial_sums = pl.pallas_call(
            pairs_kernel,
            out_shape=outgoing_shape,
            in_specs=[SMEM, VMEM, VMEM],
            out_specs=VMEM,
            scratch_shapes=[pltpu.VMEM(slot_shape, jnp.float32)],
            compiler_params=PARAMS,
            name="pair_products",
        )(pair_slots, slot_rows, cov_pairs)
        returned = exchange(partial_sums)
        outs = pl.pallas_call(
            functools.partial(update_kernel, last),
            out_shape=(whole, whole) if last else (whole, whole, whole, outgoing_shape),
            in_specs=[SMEM] * 3 + [VMEM] * (6 + len(state)),
            out_specs=(VMEM,) * (2 if last else 4),
            scratch_shapes=[pltpu.VMEM((blocks, rows, size), jnp.float32)] + ([] if last else [wire_shape]),
            compiler_params=PARAMS,
            name="update",
        )(
            served,
            break_index,
            break_levels,
            returned,
            cost_slopes,
            holdings,
            eligible,
            expected,
            cov_diag,
            *state,
        )
        if not last:
            *state, outgoing = outs
    return outs


def solution(mesh):
    placed = (
        P(("groups", "mand"), "blk"),
        P(("groups", "mand"), "blk"),
        P(("groups", "blk")),
        P(("groups", "blk"), None, None),
        P(("groups", "blk"), None, None),
        P(("groups", "blk"), None, None),
        P("groups", None, None),
        P(("groups", "blk")),
        P(),
        P(None, "mand"),
    )
    return jax.shard_map(
        body,
        mesh=mesh,
        in_specs=placed,
        out_specs=(P(("groups", "mand"), "blk"), P(("groups", "mand"), "blk")),
        check_vma=False,
    )
```

```python
import functools

import jax
import jax.numpy as jnp
from jax import lax
from jax.experimental import pallas as pl
from jax.experimental.pallas import tpu as pltpu
from jax.sharding import PartitionSpec as P

ITERS = 2
STEP_SIZE = 0.5
RISK_AVERSION = 1.0
PENALTY = 1.0

VMEM = pl.BlockSpec(memory_space=pltpu.VMEM)
SMEM = pl.BlockSpec(memory_space=pltpu.SMEM)
PARAMS = pltpu.CompilerParams(vmem_limit_bytes=24 * 1024 * 1024)


def order(owners):
    return (0, *reversed(range(1, owners)))


def fill_outgoing(served_ref, me_ref, wire_ref, outgoing):
    capacity = outgoing[0].shape[0]
    for offset, out_ref in zip(order(len(outgoing)), outgoing):
        for column_index in range(capacity):
            local = served_ref[(offset ^ me_ref[0]) * capacity + column_index]
            out_ref[column_index] = wire_ref[jnp.maximum(local, 0)]


def pack_kernel(served_ref, me_ref, holdings_ref, *refs):
    *outgoing, wire_ref = refs
    size = wire_ref.shape[2]
    for block in range(wire_ref.shape[0]):
        wire_ref[block] = holdings_ref[:, block * size : (block + 1) * size].astype(jnp.bfloat16)
    fill_outgoing(served_ref, me_ref, wire_ref, outgoing)


def pairs_kernel(owners, pairs_ref, me_ref, cov_ref, *refs):
    incoming, partial, (slot_rows, total) = refs[:owners], refs[owners : 2 * owners], refs[2 * owners :]
    capacity = incoming[0].shape[0]
    for offset, rows_ref in zip(order(owners), incoming):
        slot_rows[pl.ds(offset * capacity, capacity)] = rows_ref[...]
    total[...] = jnp.zeros_like(total)

    def place(slot):
        return ((slot // capacity) ^ me_ref[0]) * capacity + slot % capacity

    def one(pair, carry):
        first = place(pairs_ref[0, pair, 0])
        second = place(pairs_ref[0, pair, 1])
        block = cov_ref[pair]
        to_first = lax.dot_general(
            slot_rows[second], block, (((1,), (1,)), ((), ())), preferred_element_type=jnp.float32
        )
        to_second = jnp.dot(slot_rows[first], block, preferred_element_type=jnp.float32)
        total[first] += to_first
        total[second] += to_second
        return carry

    lax.fori_loop(0, cov_ref.shape[0], one, 0, unroll=16)
    for offset, out_ref in zip(order(owners), partial):
        out_ref[...] = total[pl.ds(offset * capacity, capacity)].astype(out_ref.dtype)


def column(row, rows):
    square = (rows, rows)
    on_diagonal = lax.broadcasted_iota(jnp.int32, square, 0) == lax.broadcasted_iota(jnp.int32, square, 1)
    return jnp.sum(jnp.where(on_diagonal, row, 0.0), axis=1, keepdims=True)


def update_kernel(
    last,
    owners,
    served_ref,
    me_ref,
    knee_index_ref,
    knee_levels_ref,
    slopes_ref,
    holdings_ref,
    eligible_ref,
    expected_ref,
    diag_ref,
    *refs,
):
    returned, refs = refs[:owners], refs[owners:]
    if last:
        primal_ref, traded_ref, dual_ref, traded_out, dual_out, terms = refs
    else:
        primal_out, traded_out, dual_out, *outgoing, terms, wire_ref = refs
    blocks, rows, size = terms.shape
    capacity = returned[0].shape[0]
    terms[...] = jnp.zeros_like(terms)
    for offset, back_ref in zip(order(owners), returned):
        for column_index in range(capacity):
            local = served_ref[(offset ^ me_ref[0]) * capacity + column_index]

            @pl.when(local >= 0)
            def _(local=local, back_ref=back_ref, column_index=column_index):
                terms[local] += back_ref[column_index].astype(jnp.float32)

    low = column(slopes_ref[0:1, :] / PENALTY, rows)
    high = column((slopes_ref[0:1, :] + slopes_ref[1:2, :]) / PENALTY, rows)
    for block in range(blocks):
        span = pl.ds(block * size, size)
        initial = holdings_ref[:, span]
        primal = primal_ref[:, span] if last else initial
        x_wire = primal.astype(jnp.bfloat16)
        grad = jnp.dot(x_wire, diag_ref[block], preferred_element_type=jnp.float32) + terms[block]
        expected = expected_ref[:, span]
        allowed = eligible_ref[:, span].astype(jnp.float32)
        if last:
            dual = dual_ref[:, span]
            gap = primal - traded_ref[:, span] + dual
        else:
            dual = jnp.zeros_like(initial)
            gap = dual
        primal = allowed * (primal - STEP_SIZE * (RISK_AVERSION * grad - expected + PENALTY * gap))
        shifted = primal + dual - initial
        knee = knee_levels_ref[knee_index_ref[block]]
        magnitude = jnp.abs(shifted)
        moved = jnp.minimum(jnp.maximum(magnitude - low, 0.0), knee) + jnp.maximum(
            magnitude - high - knee, 0.0
        )
        traded = initial + jnp.where(shifted < 0.0, -moved, moved)
        traded_out[:, span] = traded
        dual_out[:, span] = dual + primal - traded
        if not last:
            primal_out[:, span] = primal
            wire_ref[block] = primal.astype(jnp.bfloat16)
    if not last:
        fill_outgoing(served_ref, me_ref, wire_ref, outgoing)


def body(
    holdings,
    eligible,
    returns_mu,
    cov_diag,
    cov_pairs,
    pair_slots,
    need_table,
    break_index,
    break_levels,
    cost_slopes,
):
    rows, assets = holdings.shape
    blocks, size, _ = cov_diag.shape
    owners = lax.axis_size("blk")
    my_index = lax.axis_index("blk")
    capacity = need_table.shape[2]
    me = my_index.reshape(1)
    served = lax.dynamic_index_in_dim(need_table, my_index, 1, keepdims=False).reshape(-1)
    wire_scratch = pltpu.VMEM((blocks, rows, size), jnp.bfloat16)
    whole = jax.ShapeDtypeStruct((rows, assets), jnp.float32)
    sent = jax.ShapeDtypeStruct((capacity, rows, size), jnp.bfloat16)
    kept = jax.ShapeDtypeStruct((capacity, rows, size), jnp.float32)

    def exchange(values):
        return [values[0]] + [
            lax.ppermute(value, "blk", [(index, index ^ offset) for index in range(owners)])
            for offset, value in zip(order(owners)[1:], values[1:])
        ]

    outgoing = pl.pallas_call(
        pack_kernel,
        out_shape=[sent] * owners,
        in_specs=[SMEM, SMEM, VMEM],
        out_specs=[VMEM] * owners,
        scratch_shapes=[wire_scratch],
        compiler_params=PARAMS,
        name="pack_holdings",
    )(served, me, holdings)
    expected = returns_mu.reshape(1, assets)
    state = ()
    for iteration in range(ITERS):
        last = iteration == ITERS - 1
        incoming = exchange(outgoing)
        partial_sums = pl.pallas_call(
            functools.partial(pairs_kernel, owners),
            out_shape=[kept] + [sent] * (owners - 1),
            in_specs=[SMEM, SMEM] + [VMEM] * (1 + owners),
            out_specs=[VMEM] * owners,
            scratch_shapes=[
                pltpu.VMEM((owners * capacity, rows, size), jnp.bfloat16),
                pltpu.VMEM((owners * capacity, rows, size), jnp.float32),
            ],
            compiler_params=PARAMS,
            name="pair_products",
        )(pair_slots, me, cov_pairs, *incoming)
        returned = exchange(partial_sums)
        outs = pl.pallas_call(
            functools.partial(update_kernel, last, owners),
            out_shape=[whole] * 2 if last else [whole] * 3 + [sent] * owners,
            in_specs=[SMEM] * 4 + [VMEM] * (5 + owners + len(state)),
            out_specs=[VMEM] * (2 if last else 3 + owners),
            scratch_shapes=[pltpu.VMEM((blocks, rows, size), jnp.float32)] + ([] if last else [wire_scratch]),
            compiler_params=PARAMS,
            name="update",
        )(
            served,
            me,
            break_index,
            break_levels,
            cost_slopes,
            holdings,
            eligible,
            expected,
            cov_diag,
            *returned,
            *state,
        )
        if not last:
            state, outgoing = outs[:3], outs[3:]
    return tuple(outs)


def solution(mesh):
    placed = (
        P(("groups", "mand"), "blk"),
        P(("groups", "mand"), "blk"),
        P(("groups", "blk")),
        P(("groups", "blk"), None, None),
        P(("groups", "blk"), None, None),
        P(("groups", "blk"), None, None),
        P("groups", None, None),
        P(("groups", "blk")),
        P(),
        P(None, "mand"),
    )
    return jax.shard_map(
        body,
        mesh=mesh,
        in_specs=placed,
        out_specs=(P(("groups", "mand"), "blk"), P(("groups", "mand"), "blk")),
        check_vma=False,
    )
```

```python
import functools

import jax
import jax.numpy as jnp
from jax import lax
from jax.experimental import pallas as pl
from jax.experimental.pallas import tpu as pltpu
from jax.sharding import PartitionSpec as P

ITERS = 2
STEP_SIZE = 0.5
RISK_AVERSION = 1.0
PENALTY = 1.0

VMEM = pl.BlockSpec(memory_space=pltpu.VMEM)
SMEM = pl.BlockSpec(memory_space=pltpu.SMEM)
HBM = pl.BlockSpec(memory_space=pltpu.HBM)
PARAMS = pltpu.CompilerParams(vmem_limit_bytes=24 * 1024 * 1024)


def order(owners):
    return (0, *reversed(range(1, owners)))


def fill_outgoing(served_ref, me_ref, wire_ref, outgoing):
    capacity = outgoing[0].shape[0]
    for offset, out_ref in zip(order(len(outgoing)), outgoing):
        for column_index in range(capacity):
            local = served_ref[(offset ^ me_ref[0]) * capacity + column_index]
            out_ref[column_index] = wire_ref[jnp.maximum(local, 0)]


def pack_kernel(served_ref, me_ref, holdings_ref, *refs):
    *outgoing, wire_ref = refs
    size = wire_ref.shape[2]
    for block in range(wire_ref.shape[0]):
        wire_ref[block] = holdings_ref[:, block * size : (block + 1) * size].astype(jnp.bfloat16)
    fill_outgoing(served_ref, me_ref, wire_ref, outgoing)


def stage_kernel(cov_ref, staged_ref, sems):
    parts = sems.shape[0]
    step = cov_ref.shape[0] // parts
    copies = [
        pltpu.make_async_copy(
            cov_ref.at[pl.ds(part * step, step)], staged_ref.at[pl.ds(part * step, step)], sems.at[part]
        )
        for part in range(parts)
    ]
    for copy in copies:
        copy.start()
    for copy in copies:
        copy.wait()


def pairs_kernel(owners, pairs_ref, me_ref, cov_ref, *refs):
    incoming, partial, (slot_rows, total) = refs[:owners], refs[owners : 2 * owners], refs[2 * owners :]
    capacity = incoming[0].shape[0]
    for offset, rows_ref in zip(order(owners), incoming):
        slot_rows[pl.ds(offset * capacity, capacity)] = rows_ref[...]
    total[...] = jnp.zeros_like(total)

    def place(slot):
        return ((slot // capacity) ^ me_ref[0]) * capacity + slot % capacity

    def one(pair, carry):
        first = place(pairs_ref[0, pair, 0])
        second = place(pairs_ref[0, pair, 1])
        block = cov_ref[pair]
        to_first = lax.dot_general(
            slot_rows[second], block, (((1,), (1,)), ((), ())), preferred_element_type=jnp.float32
        )
        to_second = jnp.dot(slot_rows[first], block, preferred_element_type=jnp.float32)
        total[first] += to_first
        total[second] += to_second
        return carry

    lax.fori_loop(0, cov_ref.shape[0], one, 0, unroll=16)
    for offset, out_ref in zip(order(owners), partial):
        out_ref[...] = total[pl.ds(offset * capacity, capacity)].astype(out_ref.dtype)


def column(row, rows):
    square = (rows, rows)
    on_diagonal = lax.broadcasted_iota(jnp.int32, square, 0) == lax.broadcasted_iota(jnp.int32, square, 1)
    return jnp.sum(jnp.where(on_diagonal, row, 0.0), axis=1, keepdims=True)


def update_kernel(
    last,
    owners,
    served_ref,
    me_ref,
    knee_index_ref,
    knee_levels_ref,
    slopes_ref,
    holdings_ref,
    eligible_ref,
    expected_ref,
    diag_ref,
    *refs,
):
    returned, refs = refs[:owners], refs[owners:]
    if last:
        primal_ref, traded_ref, dual_ref, traded_out, dual_out, terms = refs
    else:
        primal_out, traded_out, dual_out, *outgoing, terms, wire_ref = refs
    blocks, rows, size = terms.shape
    capacity = returned[0].shape[0]
    terms[...] = jnp.zeros_like(terms)
    for offset, back_ref in zip(order(owners), returned):
        for column_index in range(capacity):
            local = served_ref[(offset ^ me_ref[0]) * capacity + column_index]

            @pl.when(local >= 0)
            def _(local=local, back_ref=back_ref, column_index=column_index):
                terms[local] += back_ref[column_index].astype(jnp.float32)

    low = column(slopes_ref[0:1, :] / PENALTY, rows)
    high = column((slopes_ref[0:1, :] + slopes_ref[1:2, :]) / PENALTY, rows)
    for block in range(blocks):
        span = pl.ds(block * size, size)
        initial = holdings_ref[:, span]
        primal = primal_ref[:, span] if last else initial
        x_wire = primal.astype(jnp.bfloat16)
        grad = jnp.dot(x_wire, diag_ref[block], preferred_element_type=jnp.float32) + terms[block]
        expected = expected_ref[:, span]
        allowed = eligible_ref[:, span].astype(jnp.float32)
        if last:
            dual = dual_ref[:, span]
            gap = primal - traded_ref[:, span] + dual
        else:
            dual = jnp.zeros_like(initial)
            gap = dual
        primal = allowed * (primal - STEP_SIZE * (RISK_AVERSION * grad - expected + PENALTY * gap))
        shifted = primal + dual - initial
        knee = knee_levels_ref[knee_index_ref[block]]
        magnitude = jnp.abs(shifted)
        moved = jnp.minimum(jnp.maximum(magnitude - low, 0.0), knee) + jnp.maximum(
            magnitude - high - knee, 0.0
        )
        traded = initial + jnp.where(shifted < 0.0, -moved, moved)
        traded_out[:, span] = traded
        dual_out[:, span] = dual + primal - traded
        if not last:
            primal_out[:, span] = primal
            wire_ref[block] = primal.astype(jnp.bfloat16)
    if not last:
        fill_outgoing(served_ref, me_ref, wire_ref, outgoing)


def body(
    holdings,
    eligible,
    returns_mu,
    cov_diag,
    cov_pairs,
    pair_slots,
    need_table,
    break_index,
    break_levels,
    cost_slopes,
):
    rows, assets = holdings.shape
    blocks, size, _ = cov_diag.shape
    owners = lax.axis_size("blk")
    my_index = lax.axis_index("blk")
    capacity = need_table.shape[2]
    me = my_index.reshape(1)
    served = lax.dynamic_index_in_dim(need_table, my_index, 1, keepdims=False).reshape(-1)
    wire_scratch = pltpu.VMEM((blocks, rows, size), jnp.bfloat16)
    whole = jax.ShapeDtypeStruct((rows, assets), jnp.float32)
    sent = jax.ShapeDtypeStruct((capacity, rows, size), jnp.bfloat16)
    kept = jax.ShapeDtypeStruct((capacity, rows, size), jnp.float32)

    def exchange(values):
        return [values[0]] + [
            lax.ppermute(value, "blk", [(index, index ^ offset) for index in range(owners)])
            for offset, value in zip(order(owners)[1:], values[1:])
        ]

    outgoing = pl.pallas_call(
        pack_kernel,
        out_shape=[sent] * owners,
        in_specs=[SMEM, SMEM, VMEM],
        out_specs=[VMEM] * owners,
        scratch_shapes=[wire_scratch],
        compiler_params=PARAMS,
        name="pack_holdings",
    )(served, me, holdings)
    staged = pl.pallas_call(
        stage_kernel,
        out_shape=jax.ShapeDtypeStruct(cov_pairs.shape, cov_pairs.dtype),
        in_specs=[HBM],
        out_specs=VMEM,
        scratch_shapes=[pltpu.SemaphoreType.DMA((4,))],
        compiler_params=pltpu.CompilerParams(vmem_limit_bytes=12 * 1024 * 1024),
        cost_estimate=pl.CostEstimate(flops=0, bytes_accessed=2 * cov_pairs.size, transcendentals=0),
        name="stage_pairs",
    )(cov_pairs)
    expected = returns_mu.reshape(1, assets)
    state = ()
    for iteration in range(ITERS):
        last = iteration == ITERS - 1
        incoming = exchange(outgoing)
        partial_sums = pl.pallas_call(
            functools.partial(pairs_kernel, owners),
            out_shape=[kept] + [sent] * (owners - 1),
            in_specs=[SMEM, SMEM] + [VMEM] * (1 + owners),
            out_specs=[VMEM] * owners,
            scratch_shapes=[
                pltpu.VMEM((owners * capacity, rows, size), jnp.bfloat16),
                pltpu.VMEM((owners * capacity, rows, size), jnp.float32),
            ],
            compiler_params=PARAMS,
            name="pair_products",
        )(pair_slots, me, staged, *incoming)
        returned = exchange(partial_sums)
        outs = pl.pallas_call(
            functools.partial(update_kernel, last, owners),
            out_shape=[whole] * 2 if last else [whole] * 3 + [sent] * owners,
            in_specs=[SMEM] * 4 + [VMEM] * (5 + owners + len(state)),
            out_specs=[VMEM] * (2 if last else 3 + owners),
            scratch_shapes=[pltpu.VMEM((blocks, rows, size), jnp.float32)] + ([] if last else [wire_scratch]),
            compiler_params=PARAMS,
            name="update",
        )(
            served,
            me,
            break_index,
            break_levels,
            cost_slopes,
            holdings,
            eligible,
            expected,
            cov_diag,
            *returned,
            *state,
        )
        if not last:
            state, outgoing = outs[:3], outs[3:]
    return tuple(outs)


def solution(mesh):
    placed = (
        P(("groups", "mand"), "blk"),
        P(("groups", "mand"), "blk"),
        P(("groups", "blk")),
        P(("groups", "blk"), None, None),
        P(("groups", "blk"), None, None),
        P(("groups", "blk"), None, None),
        P("groups", None, None),
        P(("groups", "blk")),
        P(),
        P(None, "mand"),
    )
    return jax.shard_map(
        body,
        mesh=mesh,
        in_specs=placed,
        out_specs=(P(("groups", "mand"), "blk"), P(("groups", "mand"), "blk")),
        check_vma=False,
    )
```

```python
import functools

import jax
import jax.numpy as jnp
from jax import lax
from jax.experimental import pallas as pl
from jax.experimental.pallas import tpu as pltpu
from jax.sharding import PartitionSpec as P

ITERS = 2
STEP_SIZE = 0.5
RISK_AVERSION = 1.0
PENALTY = 1.0

VMEM = pl.BlockSpec(memory_space=pltpu.VMEM)
SMEM = pl.BlockSpec(memory_space=pltpu.SMEM)
HBM = pl.BlockSpec(memory_space=pltpu.HBM)
PARAMS = pltpu.CompilerParams(vmem_limit_bytes=24 * 1024 * 1024)


def order(owners):
    offsets = list(reversed(range(1, owners)))
    offsets[:2] = reversed(offsets[:2])
    offsets.remove(owners // 2 - 1)
    offsets.insert(1, owners // 2 - 1)
    return (0, *offsets)


def fill_outgoing(served_ref, me_ref, wire_ref, outgoing):
    capacity = outgoing[0].shape[0]
    for offset, out_ref in zip(order(len(outgoing)), outgoing):
        for column_index in range(capacity):
            local = served_ref[(offset ^ me_ref[0]) * capacity + column_index]
            out_ref[column_index] = wire_ref[jnp.maximum(local, 0)]


def pack_kernel(served_ref, me_ref, holdings_ref, *refs):
    *outgoing, wire_ref = refs
    size = wire_ref.shape[2]
    for block in range(wire_ref.shape[0]):
        wire_ref[block] = holdings_ref[:, block * size : (block + 1) * size].astype(jnp.bfloat16)
    fill_outgoing(served_ref, me_ref, wire_ref, outgoing)


def stage_kernel(owners, capacity, cov_ref, pairs_ref, me_ref, staged_ref, places_ref, sems):
    parts = sems.shape[0]
    step = cov_ref.shape[0] // parts
    copies = [
        pltpu.make_async_copy(
            cov_ref.at[pl.ds(part * step, step)], staged_ref.at[pl.ds(part * step, step)], sems.at[part]
        )
        for part in range(parts)
    ]
    for copy in copies:
        copy.start()
    pairs, width = pairs_ref.shape[1], places_ref.shape[1]
    shape = (pairs, width)
    lane_is_pair = lax.broadcasted_iota(jnp.int32, shape, 0) == lax.broadcasted_iota(jnp.int32, shape, 1)
    offset_rank = [0] * owners
    for rank, offset in enumerate(order(owners)):
        offset_rank[offset] = rank
    places_ref[...] = jnp.zeros_like(places_ref)
    for side in range(2):
        slot = pairs_ref[0, :, side : side + 1]
        owner = lax.div(slot, jnp.full_like(slot, capacity))
        offset = owner ^ me_ref[0]
        rank = jnp.zeros_like(slot)
        for candidate in range(1, owners):
            rank = jnp.where(offset == candidate, offset_rank[candidate], rank)
        place = rank * capacity + slot - owner * capacity
        places_ref[pl.ds(side, 1), :] = jnp.sum(jnp.where(lane_is_pair, place, 0), axis=0, keepdims=True)
    for copy in copies:
        copy.wait()


def pairs_kernel(owners, places_ref, cov_ref, *refs):
    incoming, partial, (slot_rows, total) = refs[:owners], refs[owners : 2 * owners], refs[2 * owners :]
    capacity = incoming[0].shape[0]
    for rank, rows_ref in enumerate(incoming):
        slot_rows[pl.ds(rank * capacity, capacity)] = rows_ref[...]
    total[...] = jnp.zeros_like(total)

    def one(pair, carry):
        first = places_ref[0, pair]
        second = places_ref[1, pair]
        block = cov_ref[pair]
        to_first = lax.dot_general(
            slot_rows[second], block, (((1,), (1,)), ((), ())), preferred_element_type=jnp.float32
        )
        to_second = jnp.dot(slot_rows[first], block, preferred_element_type=jnp.float32)
        total[first] += to_first
        total[second] += to_second
        return carry

    lax.fori_loop(0, cov_ref.shape[0], one, 0, unroll=32)
    for rank, out_ref in enumerate(partial):
        out_ref[...] = total[pl.ds(rank * capacity, capacity)].astype(out_ref.dtype)


def column(row, rows):
    square = (rows, rows)
    on_diagonal = lax.broadcasted_iota(jnp.int32, square, 0) == lax.broadcasted_iota(jnp.int32, square, 1)
    return jnp.sum(jnp.where(on_diagonal, row, 0.0), axis=1, keepdims=True)


def update_kernel(
    last,
    owners,
    served_ref,
    me_ref,
    knee_index_ref,
    knee_levels_ref,
    slopes_ref,
    holdings_ref,
    eligible_ref,
    expected_ref,
    diag_ref,
    *refs,
):
    returned, refs = refs[:owners], refs[owners:]
    if last:
        primal_ref, traded_ref, dual_ref, traded_out, dual_out, terms = refs
    else:
        primal_out, traded_out, dual_out, *outgoing, terms, wire_ref = refs
    blocks, rows, size = terms.shape
    capacity = returned[0].shape[0]
    terms[...] = jnp.zeros_like(terms)
    for offset, back_ref in zip(order(owners), returned):
        for column_index in range(capacity):
            local = served_ref[(offset ^ me_ref[0]) * capacity + column_index]

            @pl.when(local >= 0)
            def _(local=local, back_ref=back_ref, column_index=column_index):
                terms[local] += back_ref[column_index].astype(jnp.float32)

    low = column(slopes_ref[0:1, :] / PENALTY, rows)
    high = column((slopes_ref[0:1, :] + slopes_ref[1:2, :]) / PENALTY, rows)
    for block in range(blocks):
        span = pl.ds(block * size, size)
        initial = holdings_ref[:, span]
        primal = primal_ref[:, span] if last else initial
        x_wire = primal.astype(jnp.bfloat16)
        grad = jnp.dot(x_wire, diag_ref[block], preferred_element_type=jnp.float32) + terms[block]
        expected = expected_ref[:, span]
        allowed = eligible_ref[:, span].astype(jnp.float32)
        if last:
            dual = dual_ref[:, span]
            gap = primal - traded_ref[:, span] + dual
        else:
            dual = jnp.zeros_like(initial)
            gap = dual
        primal = allowed * (primal - STEP_SIZE * (RISK_AVERSION * grad - expected + PENALTY * gap))
        shifted = primal + dual - initial
        knee = knee_levels_ref[knee_index_ref[block]]
        magnitude = jnp.abs(shifted)
        moved = jnp.minimum(jnp.maximum(magnitude - low, 0.0), knee) + jnp.maximum(
            magnitude - high - knee, 0.0
        )
        traded = initial + jnp.where(shifted < 0.0, -moved, moved)
        traded_out[:, span] = traded
        dual_out[:, span] = dual + primal - traded
        if not last:
            primal_out[:, span] = primal
            wire_ref[block] = primal.astype(jnp.bfloat16)
    if not last:
        fill_outgoing(served_ref, me_ref, wire_ref, outgoing)


def body(
    holdings,
    eligible,
    returns_mu,
    cov_diag,
    cov_pairs,
    pair_slots,
    need_table,
    break_index,
    break_levels,
    cost_slopes,
):
    rows, assets = holdings.shape
    blocks, size, _ = cov_diag.shape
    owners = lax.axis_size("blk")
    my_index = lax.axis_index("blk")
    capacity = need_table.shape[2]
    me = my_index.reshape(1)
    served = lax.dynamic_index_in_dim(need_table, my_index, 1, keepdims=False).reshape(-1)
    wire_scratch = pltpu.VMEM((blocks, rows, size), jnp.bfloat16)
    whole = jax.ShapeDtypeStruct((rows, assets), jnp.float32)
    sent = jax.ShapeDtypeStruct((capacity, rows, size), jnp.bfloat16)
    kept = jax.ShapeDtypeStruct((capacity, rows, size), jnp.float32)

    def exchange(values):
        return [values[0]] + [
            lax.ppermute(value, "blk", [(index, index ^ offset) for index in range(owners)])
            for offset, value in zip(order(owners)[1:], values[1:])
        ]

    outgoing = pl.pallas_call(
        pack_kernel,
        out_shape=[sent] * owners,
        in_specs=[SMEM, SMEM, VMEM],
        out_specs=[VMEM] * owners,
        scratch_shapes=[wire_scratch],
        compiler_params=PARAMS,
        name="pack_holdings",
    )(served, me, holdings)
    pairs = cov_pairs.shape[0]
    staged, places = pl.pallas_call(
        functools.partial(stage_kernel, owners, capacity),
        out_shape=[
            jax.ShapeDtypeStruct(cov_pairs.shape, cov_pairs.dtype),
            jax.ShapeDtypeStruct((8, -(-pairs // 128) * 128), jnp.int32),
        ],
        in_specs=[HBM, VMEM, SMEM],
        out_specs=[VMEM, VMEM],
        scratch_shapes=[pltpu.SemaphoreType.DMA((4,))],
        compiler_params=pltpu.CompilerParams(vmem_limit_bytes=12 * 1024 * 1024),
        cost_estimate=pl.CostEstimate(flops=0, bytes_accessed=2 * cov_pairs.size, transcendentals=0),
        name="stage_pairs",
    )(cov_pairs, pair_slots, me)
    expected = returns_mu.reshape(1, assets)
    state = ()
    for iteration in range(ITERS):
        last = iteration == ITERS - 1
        incoming = exchange(outgoing)
        partial_sums = pl.pallas_call(
            functools.partial(pairs_kernel, owners),
            out_shape=[kept] + [sent] * (owners - 1),
            in_specs=[SMEM] + [VMEM] * (1 + owners),
            out_specs=[VMEM] * owners,
            scratch_shapes=[
                pltpu.VMEM((owners * capacity, rows, size), jnp.bfloat16),
                pltpu.VMEM((owners * capacity, rows, size), jnp.float32),
            ],
            compiler_params=PARAMS,
            name="pair_products",
        )(places, staged, *incoming)
        returned = exchange(partial_sums)
        outs = pl.pallas_call(
            functools.partial(update_kernel, last, owners),
            out_shape=[whole] * 2 if last else [whole] * 3 + [sent] * owners,
            in_specs=[SMEM] * 4 + [VMEM] * (5 + owners + len(state)),
            out_specs=[VMEM] * (2 if last else 3 + owners),
            scratch_shapes=[pltpu.VMEM((blocks, rows, size), jnp.float32)] + ([] if last else [wire_scratch]),
            compiler_params=PARAMS,
            name="update",
        )(
            served,
            me,
            break_index,
            break_levels,
            cost_slopes,
            holdings,
            eligible,
            expected,
            cov_diag,
            *returned,
            *state,
        )
        if not last:
            state, outgoing = outs[:3], outs[3:]
    return tuple(outs)


def solution(mesh):
    placed = (
        P(("groups", "mand"), "blk"),
        P(("groups", "mand"), "blk"),
        P(("groups", "blk")),
        P(("groups", "blk"), None, None),
        P(("groups", "blk"), None, None),
        P(("groups", "blk"), None, None),
        P("groups", None, None),
        P(("groups", "blk")),
        P(),
        P(None, "mand"),
    )
    return jax.shard_map(
        body,
        mesh=mesh,
        in_specs=placed,
        out_specs=(P(("groups", "mand"), "blk"), P(("groups", "mand"), "blk")),
        check_vma=False,
    )
```

```python
import functools

import jax
import jax.numpy as jnp
from jax import lax
from jax.experimental import pallas as pl
from jax.experimental.pallas import tpu as pltpu
from jax.sharding import PartitionSpec as P

ITERS = 2
UNROLL = (16, 4, 8)
OWN = True
STEP_SIZE = 0.5
RISK_AVERSION = 1.0
PENALTY = 1.0

VMEM = pl.BlockSpec(memory_space=pltpu.VMEM)
SMEM = pl.BlockSpec(memory_space=pltpu.SMEM)
ANY = pl.BlockSpec(memory_space=pl.ANY)
HBM = pl.BlockSpec(memory_space=pltpu.HBM)
PARAMS = pltpu.CompilerParams(vmem_limit_bytes=24 * 1024 * 1024)


def order(owners):
    offsets = list(reversed(range(1, owners)))
    offsets[:2] = reversed(offsets[:2])
    offsets.remove(owners // 2 - 1)
    offsets.insert(1, owners // 2 - 1)
    return (0, *offsets)


def fill_outgoing(served_ref, me_ref, wire_ref, outgoing):
    capacity = outgoing[0].shape[0]
    for offset, out_ref in zip(order(len(outgoing)), outgoing):
        for column_index in range(capacity):
            local = served_ref[(offset ^ me_ref[0]) * capacity + column_index]
            out_ref[column_index] = wire_ref[jnp.maximum(local, 0)]


def pack_kernel(served_ref, me_ref, holdings_ref, *refs):
    *outgoing, wire_ref = refs
    size = wire_ref.shape[2]
    for block in range(wire_ref.shape[0]):
        wire_ref[block] = holdings_ref[:, block * size : (block + 1) * size].astype(jnp.bfloat16)
    fill_outgoing(served_ref, me_ref, wire_ref, outgoing)


def ranked(slot, me, owners, capacity):
    owner = lax.div(slot, jnp.full_like(slot, capacity))
    rank = jnp.zeros_like(slot)
    for candidate, offset in enumerate(order(owners)):
        rank = jnp.where(owner ^ me == offset, candidate, rank)
    return rank, rank * capacity + slot - owner * capacity


def stage_kernel(owners, capacity, cov_ref, pairs_ref, me_ref, staged_ref, places_ref, sems):
    parts = sems.shape[0]
    step = cov_ref.shape[0] // parts
    copies = [
        pltpu.make_async_copy(
            cov_ref.at[pl.ds(part * step, step)], staged_ref.at[pl.ds(part * step, step)], sems.at[part]
        )
        for part in range(parts)
    ]
    for copy in copies:
        copy.start()
    pairs, width = pairs_ref.shape[1], places_ref.shape[1]
    shape = (pairs, width)
    lane_is_pair = lax.broadcasted_iota(jnp.int32, shape, 0) == lax.broadcasted_iota(jnp.int32, shape, 1)
    places_ref[...] = jnp.zeros_like(places_ref)
    for side in range(2):
        place = ranked(pairs_ref[0, :, side : side + 1], me_ref[0], owners, capacity)[1]
        places_ref[pl.ds(side, 1), :] = jnp.sum(jnp.where(lane_is_pair, place, 0), axis=0, keepdims=True)
    for copy in copies:
        copy.wait()


def pairs_kernel(owners, places_ref, cov_ref, *refs):
    incoming, partial, (slot_rows, total) = refs[:owners], refs[owners : 2 * owners], refs[2 * owners :]
    capacity = incoming[0].shape[0]
    for rank, rows_ref in enumerate(incoming):
        slot_rows[pl.ds(rank * capacity, capacity)] = rows_ref[...]
    total[...] = jnp.zeros_like(total)

    def one(pair, carry):
        first = places_ref[0, pair]
        second = places_ref[1, pair]
        block = cov_ref[pair]
        to_first = lax.dot_general(
            slot_rows[second], block, (((1,), (1,)), ((), ())), preferred_element_type=jnp.float32
        )
        to_second = jnp.dot(slot_rows[first], block, preferred_element_type=jnp.float32)
        total[first] += to_first
        total[second] += to_second
        return carry

    lax.fori_loop(0, cov_ref.shape[0], one, 0, unroll=32)
    for rank, out_ref in enumerate(partial):
        out_ref[...] = total[pl.ds(rank * capacity, capacity)].astype(out_ref.dtype)


def plan_kernel(owners, capacity, late, pairs_ref, me_ref, after_ref, plan_ref):
    pairs, width = pairs_ref.shape[1], plan_ref.shape[1]
    slots = owners * capacity
    bits = slots.bit_length()
    shape = (pairs, width)
    pair = lax.broadcasted_iota(jnp.int32, (pairs, 1), 0)
    lane = lax.broadcasted_iota(jnp.int32, shape, 1)

    (rank0, place0), (rank1, place1) = (
        ranked(pairs_ref[0, :, side : side + 1], me_ref[0], owners, capacity) for side in range(2)
    )
    sides = []
    for side, (rank, source, target) in enumerate(((rank0, place0, place1), (rank1, place1, place0))):
        group = jnp.zeros_like(rank)
        for late_rank in late:
            group = jnp.where(rank == late_rank, 1, group)
        if OWN:
            group = jnp.where(target < capacity, 2, group)
        entry = (((pair << bits) | source) << bits) | target
        sides.append((group, entry, (lane == 2 * group + side).astype(jnp.float32)))
    square = (pairs, pairs)
    before = lax.broadcasted_iota(jnp.int32, square, 1) <= lax.broadcasted_iota(jnp.int32, square, 0)
    counts = jnp.dot(
        before.astype(jnp.bfloat16),
        (sides[0][2] + sides[1][2]).astype(jnp.bfloat16),
        preferred_element_type=jnp.float32,
    )
    for side, (group, entry, member) in enumerate(sides):
        position = jnp.sum(member * counts, axis=1, keepdims=True).astype(jnp.int32) - 1
        for index in range(3):
            listed = (position == lane) & (group == index)
            row = jnp.sum(jnp.where(listed, (entry - slots).astype(jnp.float32), 0.0), axis=0, keepdims=True)
            plan_ref[pl.ds(2 * index + side, 1), :] = row.astype(jnp.int32) + slots
    plan_ref[pl.ds(6, 1), :] = counts[pairs - 1 : pairs, :].astype(jnp.int32)
    plan_ref[pl.ds(7, 1), :] = jnp.zeros((1, width), jnp.int32)


def products(group, plan_ref, cov_ref, slot_rows, total):
    bits = slot_rows.shape[0].bit_length()
    mask = (1 << bits) - 1
    longest = jnp.maximum(plan_ref[6, 2 * group], plan_ref[6, 2 * group + 1])

    def one(step, carry):
        for lane in range(UNROLL[group]):
            for side in range(2):
                entry = plan_ref[2 * group + side, step * UNROLL[group] + lane]
                term = lax.dot_general(
                    slot_rows[(entry >> bits) & mask],
                    cov_ref[entry >> (2 * bits)],
                    (((1,), (side,)), ((), ())),
                    preferred_element_type=jnp.float32,
                )
                total[entry & mask] += term
        return carry

    lax.fori_loop(0, lax.div(longest + UNROLL[group] - 1, UNROLL[group]), one, 0)


def gather_rows(ranks, incoming, slot_rows):
    capacity = incoming[0].shape[0]
    for rank, rows_ref in zip(ranks, incoming):
        slot_rows[pl.ds(rank * capacity, capacity)] = rows_ref[...]


def early_kernel(ranks, plan_ref, cov_ref, *refs):
    *incoming, total, slot_rows = refs
    gather_rows(ranks, incoming, slot_rows)
    total[...] = jnp.zeros_like(total)
    products(0, plan_ref, cov_ref, slot_rows, total)


def late_kernel(ranks, plan_ref, cov_ref, early_ref, *refs):
    incoming, outs, (slot_rows, total) = refs[: len(ranks)], refs[len(ranks) : -2], refs[-2:]
    capacity = incoming[0].shape[0]
    gather_rows(ranks, incoming, slot_rows)
    total[...] = early_ref[...]
    products(1, plan_ref, cov_ref, slot_rows, total)
    for rank, out_ref in enumerate(outs, int(OWN)):
        out_ref[...] = total[pl.ds(rank * capacity, capacity)].astype(out_ref.dtype)


def own_kernel(owners, plan_ref, cov_ref, *refs):
    incoming, (out_ref, slot_rows, total) = refs[:owners], refs[owners:]
    capacity = incoming[0].shape[0]
    gather_rows(range(owners), incoming, slot_rows)
    total[pl.ds(0, capacity)] = jnp.zeros(out_ref.shape, jnp.float32)
    products(2, plan_ref, cov_ref, slot_rows, total)
    out_ref[...] = total[pl.ds(0, capacity)]


def column(row, rows):
    square = (rows, rows)
    on_diagonal = lax.broadcasted_iota(jnp.int32, square, 0) == lax.broadcasted_iota(jnp.int32, square, 1)
    return jnp.sum(jnp.where(on_diagonal, row, 0.0), axis=1, keepdims=True)


def update_kernel(
    last,
    owners,
    served_ref,
    me_ref,
    knee_index_ref,
    knee_levels_ref,
    slopes_ref,
    holdings_ref,
    eligible_ref,
    expected_ref,
    diag_ref,
    *refs,
):
    returned, refs = refs[:owners], refs[owners:]
    if last:
        primal_ref, traded_ref, dual_ref, traded_out, dual_out, terms = refs
    else:
        primal_out, traded_out, dual_out, *outgoing, terms, wire_ref = refs
    blocks, rows, size = terms.shape
    capacity = returned[0].shape[0]
    terms[...] = jnp.zeros_like(terms)
    for offset, back_ref in zip(order(owners), returned):
        for column_index in range(capacity):
            local = served_ref[(offset ^ me_ref[0]) * capacity + column_index]

            @pl.when(local >= 0)
            def _(local=local, back_ref=back_ref, column_index=column_index):
                terms[local] += back_ref[column_index].astype(jnp.float32)

    low = column(slopes_ref[0:1, :] / PENALTY, rows)
    high = column((slopes_ref[0:1, :] + slopes_ref[1:2, :]) / PENALTY, rows)
    for block in range(blocks):
        span = pl.ds(block * size, size)
        initial = holdings_ref[:, span]
        primal = primal_ref[:, span] if last else initial
        x_wire = primal.astype(jnp.bfloat16)
        grad = jnp.dot(x_wire, diag_ref[block], preferred_element_type=jnp.float32) + terms[block]
        expected = expected_ref[:, span]
        allowed = eligible_ref[:, span].astype(jnp.float32)
        if last:
            dual = dual_ref[:, span]
            gap = primal - traded_ref[:, span] + dual
        else:
            dual = jnp.zeros_like(initial)
            gap = dual
        primal = allowed * (primal - STEP_SIZE * (RISK_AVERSION * grad - expected + PENALTY * gap))
        shifted = primal + dual - initial
        knee = knee_levels_ref[knee_index_ref[block]]
        magnitude = jnp.abs(shifted)
        moved = jnp.minimum(jnp.maximum(magnitude - low, 0.0), knee) + jnp.maximum(
            magnitude - high - knee, 0.0
        )
        traded = initial + jnp.where(shifted < 0.0, -moved, moved)
        traded_out[:, span] = traded
        dual_out[:, span] = dual + primal - traded
        if not last:
            primal_out[:, span] = primal
            wire_ref[block] = primal.astype(jnp.bfloat16)
    if not last:
        fill_outgoing(served_ref, me_ref, wire_ref, outgoing)


def body(
    holdings,
    eligible,
    returns_mu,
    cov_diag,
    cov_pairs,
    pair_slots,
    need_table,
    break_index,
    break_levels,
    cost_slopes,
):
    rows, assets = holdings.shape
    blocks, size, _ = cov_diag.shape
    owners = lax.axis_size("blk")
    my_index = lax.axis_index("blk")
    capacity = need_table.shape[2]
    slots = owners * capacity
    pairs = cov_pairs.shape[0]
    late = tuple(rank for rank, offset in enumerate(order(owners)) if offset in (owners // 2 + 1, owners // 2))
    early = tuple(rank for rank in range(owners) if rank not in late)
    width = -(-(pairs + max(UNROLL)) // 128) * 128
    me = my_index.reshape(1)
    served = lax.dynamic_index_in_dim(need_table, my_index, 1, keepdims=False).reshape(-1)
    wire_scratch = pltpu.VMEM((blocks, rows, size), jnp.bfloat16)
    whole = jax.ShapeDtypeStruct((rows, assets), jnp.float32)
    slot_scratch = pltpu.VMEM((slots, rows, size), jnp.bfloat16)
    sent = jax.ShapeDtypeStruct((capacity, rows, size), jnp.bfloat16)
    kept = jax.ShapeDtypeStruct((capacity, rows, size), jnp.float32)

    def cost(count):
        return pl.CostEstimate(
            flops=2 * count * rows * size * size, bytes_accessed=2 * count * size * size, transcendentals=0
        )

    def exchange(values):
        return [values[0]] + [
            lax.ppermute(value, "blk", [(index, index ^ offset) for index in range(owners)])
            for offset, value in zip(order(owners)[1:], values[1:])
        ]

    outgoing = pl.pallas_call(
        pack_kernel,
        out_shape=[sent] * owners,
        in_specs=[SMEM, SMEM, VMEM],
        out_specs=[VMEM] * owners,
        scratch_shapes=[wire_scratch],
        compiler_params=PARAMS,
        name="pack_holdings",
    )(served, me, holdings)
    staged, places = pl.pallas_call(
        functools.partial(stage_kernel, owners, capacity),
        out_shape=[
            jax.ShapeDtypeStruct(cov_pairs.shape, cov_pairs.dtype),
            jax.ShapeDtypeStruct((8, -(-pairs // 128) * 128), jnp.int32),
        ],
        in_specs=[HBM, VMEM, SMEM],
        out_specs=[VMEM, VMEM],
        scratch_shapes=[pltpu.SemaphoreType.DMA((4,))],
        compiler_params=pltpu.CompilerParams(vmem_limit_bytes=12 * 1024 * 1024),
        cost_estimate=pl.CostEstimate(flops=0, bytes_accessed=2 * cov_pairs.size, transcendentals=0),
        name="stage_pairs",
    )(cov_pairs, pair_slots, me)
    expected = returns_mu.reshape(1, assets)
    state = ()
    for iteration in range(ITERS):
        last = iteration == ITERS - 1
        incoming = exchange(outgoing)
        if iteration == 0:
            partial_sums = pl.pallas_call(
                functools.partial(pairs_kernel, owners),
                out_shape=[kept] + [sent] * (owners - 1),
                in_specs=[SMEM] + [VMEM] * (1 + owners),
                out_specs=[VMEM] * owners,
                scratch_shapes=[
                    pltpu.VMEM((owners * capacity, rows, size), jnp.bfloat16),
                    pltpu.VMEM((owners * capacity, rows, size), jnp.float32),
                ],
                compiler_params=PARAMS,
                name="pair_products",
            )(places, staged, *incoming)
            plan = pl.pallas_call(
                functools.partial(plan_kernel, owners, capacity, late),
                out_shape=jax.ShapeDtypeStruct((8, width), jnp.int32),
                in_specs=[VMEM, SMEM, ANY],
                out_specs=VMEM,
                compiler_params=PARAMS,
                cost_estimate=pl.CostEstimate(flops=0, bytes_accessed=1 << 20, transcendentals=0),
                name="plan_products",
            )(pair_slots, me, partial_sums[0])
        else:
            total_shape = (slots + 1, rows, size)
            total = pl.pallas_call(
                functools.partial(early_kernel, early),
                out_shape=jax.ShapeDtypeStruct(total_shape, jnp.float32),
                in_specs=[SMEM] + [VMEM] * (1 + len(early)),
                out_specs=VMEM,
                scratch_shapes=[slot_scratch],
                compiler_params=PARAMS,
                cost_estimate=cost(pairs),
                name="early_products",
            )(plan, cov_pairs, *(incoming[rank] for rank in early))
            partial_sums = pl.pallas_call(
                functools.partial(late_kernel, late),
                out_shape=([] if OWN else [kept]) + [sent] * (owners - 1),
                in_specs=[SMEM] + [VMEM] * (2 + len(late)),
                out_specs=[VMEM] * (owners - int(OWN)),
                scratch_shapes=[slot_scratch, pltpu.VMEM(total_shape, jnp.float32)],
                compiler_params=PARAMS,
                cost_estimate=cost(pairs),
                name="late_products",
            )(plan, cov_pairs, total, *(incoming[rank] for rank in late))
            if OWN:
                own = pl.pallas_call(
                    functools.partial(own_kernel, owners),
                    out_shape=kept,
                    in_specs=[SMEM] + [VMEM] * (1 + owners),
                    out_specs=VMEM,
                    scratch_shapes=[slot_scratch, pltpu.VMEM(total_shape, jnp.float32)],
                    compiler_params=PARAMS,
                    cost_estimate=cost(pairs // 2),
                    name="own_products",
                )(plan, cov_pairs, *incoming)
                partial_sums = [own, *partial_sums]
        returned = exchange(partial_sums)
        outs = pl.pallas_call(
            functools.partial(update_kernel, last, owners),
            out_shape=[whole] * 2 if last else [whole] * 3 + [sent] * owners,
            in_specs=[SMEM] * 4 + [VMEM] * (5 + owners + len(state)),
            out_specs=[VMEM] * (2 if last else 3 + owners),
            scratch_shapes=[pltpu.VMEM((blocks, rows, size), jnp.float32)] + ([] if last else [wire_scratch]),
            compiler_params=PARAMS,
            name="update",
        )(
            served,
            me,
            break_index,
            break_levels,
            cost_slopes,
            holdings,
            eligible,
            expected,
            cov_diag,
            *returned,
            *state,
        )
        if not last:
            state, outgoing = outs[:3], outs[3:]
    return tuple(outs)


def solution(mesh):
    placed = (
        P(("groups", "mand"), "blk"),
        P(("groups", "mand"), "blk"),
        P(("groups", "blk")),
        P(("groups", "blk"), None, None),
        P(("groups", "blk"), None, None),
        P(("groups", "blk"), None, None),
        P("groups", None, None),
        P(("groups", "blk")),
        P(),
        P(None, "mand"),
    )
    return jax.shard_map(
        body,
        mesh=mesh,
        in_specs=placed,
        out_specs=(P(("groups", "mand"), "blk"), P(("groups", "mand"), "blk")),
        check_vma=False,
    )
```

```python
import functools

import jax
import jax.numpy as jnp
from jax import lax
from jax.experimental import pallas as pl
from jax.experimental.pallas import tpu as pltpu
from jax.sharding import PartitionSpec as P

ITERS = 2
LANES = 8
LANES_LEFT = 4
OWN = True
STEP_SIZE = 0.5
RISK_AVERSION = 1.0
PENALTY = 1.0

VMEM = pl.BlockSpec(memory_space=pltpu.VMEM)
SMEM = pl.BlockSpec(memory_space=pltpu.SMEM)
ANY = pl.BlockSpec(memory_space=pl.ANY)
HBM = pl.BlockSpec(memory_space=pltpu.HBM)
PARAMS = pltpu.CompilerParams(vmem_limit_bytes=24 * 1024 * 1024)


def order(owners):
    offsets = list(reversed(range(1, owners)))
    offsets[:2] = reversed(offsets[:2])
    for place, offset in ((1, owners // 2 - 1), (3, owners // 2 - 2)):
        offsets.remove(offset)
        offsets.insert(place, offset)
    return (0, *offsets)


def fill_outgoing(served_ref, me_ref, wire_ref, outgoing):
    capacity = outgoing[0].shape[0]
    for offset, out_ref in zip(order(len(outgoing)), outgoing):
        for column_index in range(capacity):
            local = served_ref[(offset ^ me_ref[0]) * capacity + column_index]
            out_ref[column_index] = wire_ref[jnp.maximum(local, 0)]


def pack_kernel(served_ref, me_ref, holdings_ref, *refs):
    *outgoing, wire_ref = refs
    size = wire_ref.shape[2]
    for block in range(wire_ref.shape[0]):
        wire_ref[block] = holdings_ref[:, block * size : (block + 1) * size].astype(jnp.bfloat16)
    fill_outgoing(served_ref, me_ref, wire_ref, outgoing)


def ranked(slot, me, owners, capacity):
    owner = lax.div(slot, jnp.full_like(slot, capacity))
    rank = jnp.zeros_like(slot)
    for candidate, offset in enumerate(order(owners)):
        rank = jnp.where(owner ^ me == offset, candidate, rank)
    return rank, rank * capacity + slot - owner * capacity


def stage_kernel(owners, capacity, cov_ref, pairs_ref, me_ref, staged_ref, places_ref, sems):
    parts = sems.shape[0]
    step = cov_ref.shape[0] // parts
    copies = [
        pltpu.make_async_copy(
            cov_ref.at[pl.ds(part * step, step)], staged_ref.at[pl.ds(part * step, step)], sems.at[part]
        )
        for part in range(parts)
    ]
    for copy in copies:
        copy.start()
    pairs, width = pairs_ref.shape[1], places_ref.shape[1]
    shape = (pairs, width)
    lane_is_pair = lax.broadcasted_iota(jnp.int32, shape, 0) == lax.broadcasted_iota(jnp.int32, shape, 1)
    places_ref[...] = jnp.zeros_like(places_ref)
    for side in range(2):
        place = ranked(pairs_ref[0, :, side : side + 1], me_ref[0], owners, capacity)[1]
        places_ref[pl.ds(side, 1), :] = jnp.sum(jnp.where(lane_is_pair, place, 0), axis=0, keepdims=True)
    for copy in copies:
        copy.wait()


def pairs_kernel(owners, places_ref, cov_ref, *refs):
    incoming, partial, (slot_rows, total) = refs[:owners], refs[owners : 2 * owners], refs[2 * owners :]
    capacity = incoming[0].shape[0]
    for rank, rows_ref in enumerate(incoming):
        slot_rows[pl.ds(rank * capacity, capacity)] = rows_ref[...]
    total[...] = jnp.zeros_like(total)

    def one(pair, carry):
        first = places_ref[0, pair]
        second = places_ref[1, pair]
        block = cov_ref[pair]
        to_first = lax.dot_general(
            slot_rows[second], block, (((1,), (1,)), ((), ())), preferred_element_type=jnp.float32
        )
        to_second = jnp.dot(slot_rows[first], block, preferred_element_type=jnp.float32)
        total[first] += to_first
        total[second] += to_second
        return carry

    lax.fori_loop(0, cov_ref.shape[0], one, 0, unroll=32)
    for rank, out_ref in enumerate(partial):
        out_ref[...] = total[pl.ds(rank * capacity, capacity)].astype(out_ref.dtype)


def plan_kernel(owners, capacity, late, pairs_ref, me_ref, after_ref, plan_ref):
    pairs, width = pairs_ref.shape[1], plan_ref.shape[1]
    slots = owners * capacity
    bits = slots.bit_length()
    shape = (pairs, width)
    pair = lax.broadcasted_iota(jnp.int32, (pairs, 1), 0)
    lane = lax.broadcasted_iota(jnp.int32, shape, 1)

    (rank0, place0), (rank1, place1) = (
        ranked(pairs_ref[0, :, side : side + 1], me_ref[0], owners, capacity) for side in range(2)
    )
    sides = []
    for side, (rank, source, target) in enumerate(((rank0, place0, place1), (rank1, place1, place0))):
        group = jnp.zeros_like(rank)
        for late_rank in late:
            group = jnp.where(rank == late_rank, 1, group)
        if OWN:
            group = jnp.where(target < capacity, 2, group)
        entry = (((pair << bits) | source) << bits) | target
        sides.append((group, entry, (lane == 2 * group + side).astype(jnp.float32)))
    square = (pairs, pairs)
    before = lax.broadcasted_iota(jnp.int32, square, 1) <= lax.broadcasted_iota(jnp.int32, square, 0)
    counts = jnp.dot(
        before.astype(jnp.bfloat16),
        (sides[0][2] + sides[1][2]).astype(jnp.bfloat16),
        preferred_element_type=jnp.float32,
    )
    for side, (group, entry, member) in enumerate(sides):
        position = jnp.sum(member * counts, axis=1, keepdims=True).astype(jnp.int32) - 1
        for index in range(3):
            listed = (position == lane) & (group == index)
            row = jnp.sum(jnp.where(listed, (entry - slots).astype(jnp.float32), 0.0), axis=0, keepdims=True)
            plan_ref[pl.ds(2 * index + side, 1), :] = row.astype(jnp.int32) + slots
    plan_ref[pl.ds(6, 1), :] = counts[pairs - 1 : pairs, :].astype(jnp.int32)
    plan_ref[pl.ds(7, 1), :] = jnp.zeros((1, width), jnp.int32)


def products(group, plan_ref, cov_ref, slot_rows, total):
    bits = slot_rows.shape[0].bit_length()
    mask = (1 << bits) - 1
    longest = jnp.maximum(plan_ref[6, 2 * group], plan_ref[6, 2 * group + 1])

    def steps(start, lanes):
        def one(step, carry):
            for lane in range(lanes):
                for side in range(2):
                    entry = plan_ref[2 * group + side, start + step * lanes + lane]
                    term = lax.dot_general(
                        slot_rows[(entry >> bits) & mask],
                        cov_ref[entry >> (2 * bits)],
                        (((1,), (side,)), ((), ())),
                        preferred_element_type=jnp.float32,
                    )
                    total[entry & mask] += term
            return carry

        return one

    whole = lax.div(longest, LANES)
    done = whole * LANES
    lax.fori_loop(0, whole, steps(0, LANES), 0)
    lax.fori_loop(0, lax.div(longest - done + LANES_LEFT - 1, LANES_LEFT), steps(done, LANES_LEFT), 0)


def gather_rows(ranks, incoming, slot_rows):
    capacity = incoming[0].shape[0]
    for rank, rows_ref in zip(ranks, incoming):
        slot_rows[pl.ds(rank * capacity, capacity)] = rows_ref[...]


def early_kernel(ranks, plan_ref, cov_ref, *refs):
    *incoming, total, slot_rows = refs
    gather_rows(ranks, incoming, slot_rows)
    total[...] = jnp.zeros_like(total)
    products(0, plan_ref, cov_ref, slot_rows, total)


def late_kernel(ranks, plan_ref, cov_ref, early_ref, *refs):
    incoming, outs, (slot_rows, total) = refs[: len(ranks)], refs[len(ranks) : -2], refs[-2:]
    capacity = incoming[0].shape[0]
    gather_rows(ranks, incoming, slot_rows)
    total[...] = early_ref[...]
    products(1, plan_ref, cov_ref, slot_rows, total)
    for rank, out_ref in enumerate(outs, int(OWN)):
        out_ref[...] = total[pl.ds(rank * capacity, capacity)].astype(out_ref.dtype)


def own_kernel(owners, plan_ref, cov_ref, *refs):
    incoming, (out_ref, slot_rows, total) = refs[:owners], refs[owners:]
    capacity = incoming[0].shape[0]
    gather_rows(range(owners), incoming, slot_rows)
    total[pl.ds(0, capacity)] = jnp.zeros(out_ref.shape, jnp.float32)
    products(2, plan_ref, cov_ref, slot_rows, total)
    out_ref[...] = total[pl.ds(0, capacity)]


def column(row, rows):
    square = (rows, rows)
    on_diagonal = lax.broadcasted_iota(jnp.int32, square, 0) == lax.broadcasted_iota(jnp.int32, square, 1)
    return jnp.sum(jnp.where(on_diagonal, row, 0.0), axis=1, keepdims=True)


def update_kernel(
    last,
    owners,
    served_ref,
    me_ref,
    knee_index_ref,
    knee_levels_ref,
    slopes_ref,
    holdings_ref,
    eligible_ref,
    expected_ref,
    diag_ref,
    *refs,
):
    returned, refs = refs[:owners], refs[owners:]
    if last:
        primal_ref, traded_ref, dual_ref, traded_out, dual_out, terms = refs
    else:
        primal_out, traded_out, dual_out, *outgoing, terms, wire_ref = refs
    blocks, rows, size = terms.shape
    capacity = returned[0].shape[0]
    terms[...] = jnp.zeros_like(terms)
    for offset, back_ref in zip(order(owners), returned):
        for column_index in range(capacity):
            local = served_ref[(offset ^ me_ref[0]) * capacity + column_index]

            @pl.when(local >= 0)
            def _(local=local, back_ref=back_ref, column_index=column_index):
                terms[local] += back_ref[column_index].astype(jnp.float32)

    low = column(slopes_ref[0:1, :] / PENALTY, rows)
    high = column((slopes_ref[0:1, :] + slopes_ref[1:2, :]) / PENALTY, rows)
    for block in range(blocks):
        span = pl.ds(block * size, size)
        initial = holdings_ref[:, span]
        primal = primal_ref[:, span] if last else initial
        x_wire = primal.astype(jnp.bfloat16)
        grad = jnp.dot(x_wire, diag_ref[block], preferred_element_type=jnp.float32) + terms[block]
        expected = expected_ref[:, span]
        allowed = eligible_ref[:, span].astype(jnp.float32)
        if last:
            dual = dual_ref[:, span]
            gap = primal - traded_ref[:, span] + dual
        else:
            dual = jnp.zeros_like(initial)
            gap = dual
        primal = allowed * (primal - STEP_SIZE * (RISK_AVERSION * grad - expected + PENALTY * gap))
        shifted = primal + dual - initial
        knee = knee_levels_ref[knee_index_ref[block]]
        magnitude = jnp.abs(shifted)
        moved = jnp.minimum(jnp.maximum(magnitude - low, 0.0), knee) + jnp.maximum(
            magnitude - high - knee, 0.0
        )
        traded = initial + jnp.where(shifted < 0.0, -moved, moved)
        traded_out[:, span] = traded
        dual_out[:, span] = dual + primal - traded
        if not last:
            primal_out[:, span] = primal
            wire_ref[block] = primal.astype(jnp.bfloat16)
    if not last:
        fill_outgoing(served_ref, me_ref, wire_ref, outgoing)


def body(
    holdings,
    eligible,
    returns_mu,
    cov_diag,
    cov_pairs,
    pair_slots,
    need_table,
    break_index,
    break_levels,
    cost_slopes,
):
    rows, assets = holdings.shape
    blocks, size, _ = cov_diag.shape
    owners = lax.axis_size("blk")
    my_index = lax.axis_index("blk")
    capacity = need_table.shape[2]
    slots = owners * capacity
    pairs = cov_pairs.shape[0]
    late = tuple(rank for rank, offset in enumerate(order(owners)) if offset in (owners // 2 + 1, owners // 2))
    early = tuple(rank for rank in range(owners) if rank not in late)
    width = -(-(pairs + LANES) // 128) * 128
    me = my_index.reshape(1)
    served = lax.dynamic_index_in_dim(need_table, my_index, 1, keepdims=False).reshape(-1)
    wire_scratch = pltpu.VMEM((blocks, rows, size), jnp.bfloat16)
    whole = jax.ShapeDtypeStruct((rows, assets), jnp.float32)
    slot_scratch = pltpu.VMEM((slots, rows, size), jnp.bfloat16)
    sent = jax.ShapeDtypeStruct((capacity, rows, size), jnp.bfloat16)
    kept = jax.ShapeDtypeStruct((capacity, rows, size), jnp.float32)

    def cost(count):
        return pl.CostEstimate(
            flops=2 * count * rows * size * size, bytes_accessed=2 * count * size * size, transcendentals=0
        )

    def exchange(values):
        return [values[0]] + [
            lax.ppermute(value, "blk", [(index, index ^ offset) for index in range(owners)])
            for offset, value in zip(order(owners)[1:], values[1:])
        ]

    outgoing = pl.pallas_call(
        pack_kernel,
        out_shape=[sent] * owners,
        in_specs=[SMEM, SMEM, VMEM],
        out_specs=[VMEM] * owners,
        scratch_shapes=[wire_scratch],
        compiler_params=PARAMS,
        cost_estimate=pl.CostEstimate(flops=10**11, bytes_accessed=64 << 20, transcendentals=10**8),
        name="pack_holdings",
    )(served, me, holdings)
    staged, places = pl.pallas_call(
        functools.partial(stage_kernel, owners, capacity),
        out_shape=[
            jax.ShapeDtypeStruct(cov_pairs.shape, cov_pairs.dtype),
            jax.ShapeDtypeStruct((8, -(-pairs // 128) * 128), jnp.int32),
        ],
        in_specs=[HBM, VMEM, SMEM],
        out_specs=[VMEM, VMEM],
        scratch_shapes=[pltpu.SemaphoreType.DMA((4,))],
        compiler_params=pltpu.CompilerParams(vmem_limit_bytes=12 * 1024 * 1024),
        cost_estimate=pl.CostEstimate(flops=0, bytes_accessed=2 * cov_pairs.size, transcendentals=0),
        name="stage_pairs",
    )(cov_pairs, pair_slots, me)
    expected = returns_mu.reshape(1, assets)
    state = ()
    for iteration in range(ITERS):
        last = iteration == ITERS - 1
        incoming = exchange(outgoing)
        if iteration == 0:
            partial_sums = pl.pallas_call(
                functools.partial(pairs_kernel, owners),
                out_shape=[kept] + [sent] * (owners - 1),
                in_specs=[SMEM] + [VMEM] * (1 + owners),
                out_specs=[VMEM] * owners,
                scratch_shapes=[
                    pltpu.VMEM((owners * capacity, rows, size), jnp.bfloat16),
                    pltpu.VMEM((owners * capacity, rows, size), jnp.float32),
                ],
                compiler_params=PARAMS,
                name="pair_products",
            )(places, staged, *incoming)
            plan = pl.pallas_call(
                functools.partial(plan_kernel, owners, capacity, late),
                out_shape=jax.ShapeDtypeStruct((8, width), jnp.int32),
                in_specs=[VMEM, SMEM, ANY],
                out_specs=VMEM,
                compiler_params=PARAMS,
                cost_estimate=pl.CostEstimate(flops=0, bytes_accessed=1 << 20, transcendentals=0),
                name="plan_products",
            )(pair_slots, me, partial_sums[0])
        else:
            total_shape = (slots + 1, rows, size)
            total = pl.pallas_call(
                functools.partial(early_kernel, early),
                out_shape=jax.ShapeDtypeStruct(total_shape, jnp.float32),
                in_specs=[SMEM] + [VMEM] * (1 + len(early)),
                out_specs=VMEM,
                scratch_shapes=[slot_scratch],
                compiler_params=PARAMS,
                cost_estimate=cost(pairs),
                name="early_products",
            )(plan, cov_pairs, *(incoming[rank] for rank in early))
            partial_sums = pl.pallas_call(
                functools.partial(late_kernel, late),
                out_shape=([] if OWN else [kept]) + [sent] * (owners - 1),
                in_specs=[SMEM] + [VMEM] * (2 + len(late)),
                out_specs=[VMEM] * (owners - int(OWN)),
                scratch_shapes=[slot_scratch, pltpu.VMEM(total_shape, jnp.float32)],
                compiler_params=PARAMS,
                cost_estimate=cost(pairs),
                name="late_products",
            )(plan, cov_pairs, total, *(incoming[rank] for rank in late))
            if OWN:
                own = pl.pallas_call(
                    functools.partial(own_kernel, owners),
                    out_shape=kept,
                    in_specs=[SMEM] + [VMEM] * (1 + owners),
                    out_specs=VMEM,
                    scratch_shapes=[slot_scratch, pltpu.VMEM(total_shape, jnp.float32)],
                    compiler_params=PARAMS,
                    cost_estimate=cost(pairs // 2),
                    name="own_products",
                )(plan, cov_pairs, *incoming)
                partial_sums = [own, *partial_sums]
        returned = exchange(partial_sums)
        outs = pl.pallas_call(
            functools.partial(update_kernel, last, owners),
            out_shape=[whole] * 2 if last else [whole] * 3 + [sent] * owners,
            in_specs=[SMEM] * 4 + [VMEM] * (5 + owners + len(state)),
            out_specs=[VMEM] * (2 if last else 3 + owners),
            scratch_shapes=[pltpu.VMEM((blocks, rows, size), jnp.float32)] + ([] if last else [wire_scratch]),
            compiler_params=PARAMS,
            name="update",
        )(
            served,
            me,
            break_index,
            break_levels,
            cost_slopes,
            holdings,
            eligible,
            expected,
            cov_diag,
            *returned,
            *state,
        )
        if not last:
            state, outgoing = outs[:3], outs[3:]
    return tuple(outs)


def solution(mesh):
    placed = (
        P(("groups", "mand"), "blk"),
        P(("groups", "mand"), "blk"),
        P(("groups", "blk")),
        P(("groups", "blk"), None, None),
        P(("groups", "blk"), None, None),
        P(("groups", "blk"), None, None),
        P("groups", None, None),
        P(("groups", "blk")),
        P(),
        P(None, "mand"),
    )
    return jax.shard_map(
        body,
        mesh=mesh,
        in_specs=placed,
        out_specs=(P(("groups", "mand"), "blk"), P(("groups", "mand"), "blk")),
        check_vma=False,
    )
```

```python
import functools

import jax
import jax.numpy as jnp
from jax import lax
from jax.experimental import pallas as pl
from jax.experimental.pallas import tpu as pltpu
from jax.sharding import PartitionSpec as P

ITERS = 2
LANES = 8
LANES_LEFT = 4
OWN = True
STEP_SIZE = 0.5
RISK_AVERSION = 1.0
PENALTY = 1.0

VMEM = pl.BlockSpec(memory_space=pltpu.VMEM)
SMEM = pl.BlockSpec(memory_space=pltpu.SMEM)
ANY = pl.BlockSpec(memory_space=pl.ANY)
HBM = pl.BlockSpec(memory_space=pltpu.HBM)
PARAMS = pltpu.CompilerParams(vmem_limit_bytes=24 * 1024 * 1024)


def order(owners):
    offsets = list(reversed(range(1, owners)))
    offsets[:2] = reversed(offsets[:2])
    for place, offset in ((1, owners // 2 - 1), (3, owners // 2 - 2)):
        offsets.remove(offset)
        offsets.insert(place, offset)
    return (0, *offsets)


def fill_outgoing(served_ref, me_ref, wire_ref, outgoing):
    capacity = outgoing[0].shape[0]
    for offset, out_ref in zip(order(len(outgoing)), outgoing):
        for column_index in range(capacity):
            local = served_ref[(offset ^ me_ref[0]) * capacity + column_index]
            out_ref[column_index] = wire_ref[jnp.maximum(local, 0)]


def pack_kernel(served_ref, me_ref, holdings_ref, *refs):
    *outgoing, wire_ref = refs
    size = wire_ref.shape[2]
    for block in range(wire_ref.shape[0]):
        wire_ref[block] = holdings_ref[:, block * size : (block + 1) * size].astype(jnp.bfloat16)
    fill_outgoing(served_ref, me_ref, wire_ref, outgoing)


def ranked(slot, me, owners, capacity):
    owner = lax.div(slot, jnp.full_like(slot, capacity))
    rank = jnp.zeros_like(slot)
    for candidate, offset in enumerate(order(owners)):
        rank = jnp.where(owner ^ me == offset, candidate, rank)
    return rank, rank * capacity + slot - owner * capacity


def stage_kernel(owners, capacity, cov_ref, pairs_ref, me_ref, staged_ref, places_ref, sems):
    parts = sems.shape[0]
    step = cov_ref.shape[0] // parts
    copies = [
        pltpu.make_async_copy(
            cov_ref.at[pl.ds(part * step, step)], staged_ref.at[pl.ds(part * step, step)], sems.at[part]
        )
        for part in range(parts)
    ]
    for copy in copies:
        copy.start()
    pairs, width = pairs_ref.shape[1], places_ref.shape[1]
    shape = (pairs, width)
    lane_is_pair = lax.broadcasted_iota(jnp.int32, shape, 0) == lax.broadcasted_iota(jnp.int32, shape, 1)
    places_ref[...] = jnp.zeros_like(places_ref)
    for side in range(2):
        place = ranked(pairs_ref[0, :, side : side + 1], me_ref[0], owners, capacity)[1]
        places_ref[pl.ds(side, 1), :] = jnp.sum(jnp.where(lane_is_pair, place, 0), axis=0, keepdims=True)
    for copy in copies:
        copy.wait()


def pairs_kernel(owners, places_ref, cov_ref, *refs):
    incoming, partial, (slot_rows, total) = refs[:owners], refs[owners : 2 * owners], refs[2 * owners :]
    capacity = incoming[0].shape[0]
    for rank, rows_ref in enumerate(incoming):
        slot_rows[pl.ds(rank * capacity, capacity)] = rows_ref[...]
    total[...] = jnp.zeros_like(total)

    def one(pair, carry):
        first = places_ref[0, pair]
        second = places_ref[1, pair]
        block = cov_ref[pair]
        to_first = lax.dot_general(
            slot_rows[second], block, (((1,), (1,)), ((), ())), preferred_element_type=jnp.float32
        )
        to_second = jnp.dot(slot_rows[first], block, preferred_element_type=jnp.float32)
        total[first] += to_first
        total[second] += to_second
        return carry

    lax.fori_loop(0, cov_ref.shape[0], one, 0, unroll=32)
    for rank, out_ref in enumerate(partial):
        out_ref[...] = total[pl.ds(rank * capacity, capacity)].astype(out_ref.dtype)


def plan_kernel(owners, capacity, late, pairs_ref, me_ref, after_ref, plan_ref):
    pairs, width = pairs_ref.shape[1], plan_ref.shape[1]
    slots = owners * capacity
    bits = slots.bit_length()
    shape = (pairs, width)
    pair = lax.broadcasted_iota(jnp.int32, (pairs, 1), 0)
    lane = lax.broadcasted_iota(jnp.int32, shape, 1)

    (rank0, place0), (rank1, place1) = (
        ranked(pairs_ref[0, :, side : side + 1], me_ref[0], owners, capacity) for side in range(2)
    )
    sides = []
    for side, (rank, source, target) in enumerate(((rank0, place0, place1), (rank1, place1, place0))):
        group = jnp.zeros_like(rank)
        for late_rank in late:
            group = jnp.where(rank == late_rank, 1, group)
        if OWN:
            group = jnp.where(target < capacity, 2, group)
        entry = (((pair << bits) | source) << bits) | target
        sides.append((group, entry, (lane == 2 * group + side).astype(jnp.float32)))
    square = (pairs, pairs)
    before = lax.broadcasted_iota(jnp.int32, square, 1) <= lax.broadcasted_iota(jnp.int32, square, 0)
    counts = jnp.dot(
        before.astype(jnp.bfloat16),
        (sides[0][2] + sides[1][2]).astype(jnp.bfloat16),
        preferred_element_type=jnp.float32,
    )
    for side, (group, entry, member) in enumerate(sides):
        position = jnp.sum(member * counts, axis=1, keepdims=True).astype(jnp.int32) - 1
        for index in range(3):
            listed = (position == lane) & (group == index)
            row = jnp.sum(jnp.where(listed, (entry - slots).astype(jnp.float32), 0.0), axis=0, keepdims=True)
            plan_ref[pl.ds(2 * index + side, 1), :] = row.astype(jnp.int32) + slots
    plan_ref[pl.ds(6, 1), :] = counts[pairs - 1 : pairs, :].astype(jnp.int32)
    plan_ref[pl.ds(7, 1), :] = jnp.zeros((1, width), jnp.int32)


def products(group, plan_ref, cov_ref, slot_rows, total):
    bits = slot_rows.shape[0].bit_length()
    mask = (1 << bits) - 1
    longest = jnp.maximum(plan_ref[6, 2 * group], plan_ref[6, 2 * group + 1])

    def steps(start, lanes):
        def one(step, carry):
            for lane in range(lanes):
                for side in range(2):
                    entry = plan_ref[2 * group + side, start + step * lanes + lane]
                    term = lax.dot_general(
                        slot_rows[(entry >> bits) & mask],
                        cov_ref[entry >> (2 * bits)],
                        (((1,), (side,)), ((), ())),
                        preferred_element_type=jnp.float32,
                    )
                    total[entry & mask] += term
            return carry

        return one

    whole = lax.div(longest, LANES)
    done = whole * LANES
    lax.fori_loop(0, whole, steps(0, LANES), 0)
    lax.fori_loop(0, lax.div(longest - done + LANES_LEFT - 1, LANES_LEFT), steps(done, LANES_LEFT), 0)


def gather_rows(ranks, incoming, slot_rows):
    capacity = incoming[0].shape[0]
    for rank, rows_ref in zip(ranks, incoming):
        slot_rows[pl.ds(rank * capacity, capacity)] = rows_ref[...]


def early_kernel(ranks, plan_ref, cov_ref, *refs):
    *incoming, total, slot_rows = refs
    gather_rows(ranks, incoming, slot_rows)
    total[...] = jnp.zeros_like(total)
    products(0, plan_ref, cov_ref, slot_rows, total)


def late_kernel(ranks, plan_ref, cov_ref, early_ref, *refs):
    incoming, outs, (slot_rows, total) = refs[: len(ranks)], refs[len(ranks) : -2], refs[-2:]
    capacity = incoming[0].shape[0]
    gather_rows(ranks, incoming, slot_rows)
    total[...] = early_ref[...]
    products(1, plan_ref, cov_ref, slot_rows, total)
    for rank, out_ref in enumerate(outs, int(OWN)):
        out_ref[...] = total[pl.ds(rank * capacity, capacity)].astype(out_ref.dtype)


def own_kernel(owners, plan_ref, cov_ref, *refs):
    incoming, (out_ref, slot_rows, total) = refs[:owners], refs[owners:]
    capacity = incoming[0].shape[0]
    gather_rows(range(owners), incoming, slot_rows)
    total[pl.ds(0, capacity)] = jnp.zeros(out_ref.shape, jnp.float32)
    products(2, plan_ref, cov_ref, slot_rows, total)
    out_ref[...] = total[pl.ds(0, capacity)]


def column(row, rows):
    square = (rows, rows)
    on_diagonal = lax.broadcasted_iota(jnp.int32, square, 0) == lax.broadcasted_iota(jnp.int32, square, 1)
    return jnp.sum(jnp.where(on_diagonal, row, 0.0), axis=1, keepdims=True)


def add_returned(served_ref, me_ref, offsets, returned, terms):
    capacity = returned[0].shape[0]
    for offset, back_ref in zip(offsets, returned):
        for column_index in range(capacity):
            local = served_ref[(offset ^ me_ref[0]) * capacity + column_index]

            @pl.when(local >= 0)
            def _(local=local, back_ref=back_ref, column_index=column_index):
                terms[local] += back_ref[column_index].astype(jnp.float32)


def terms_kernel(offsets, served_ref, me_ref, diag_ref, primal_ref, *refs):
    *returned, terms = refs
    blocks, _, size = terms.shape
    for block in range(blocks):
        x_wire = primal_ref[:, block * size : (block + 1) * size].astype(jnp.bfloat16)
        terms[block] = jnp.dot(x_wire, diag_ref[block], preferred_element_type=jnp.float32)
    add_returned(served_ref, me_ref, offsets, returned, terms)


def update_kernel(
    last,
    offsets,
    served_ref,
    me_ref,
    knee_index_ref,
    knee_levels_ref,
    slopes_ref,
    holdings_ref,
    eligible_ref,
    expected_ref,
    terms_ref,
    *refs,
):
    returned, refs = refs[: len(offsets)], refs[len(offsets) :]
    if last:
        primal_ref, traded_ref, dual_ref, traded_out, dual_out, terms = refs
    else:
        primal_out, traded_out, dual_out, *outgoing, terms, wire_ref = refs
    blocks, rows, size = terms.shape
    terms[...] = terms_ref[...]
    add_returned(served_ref, me_ref, offsets, returned, terms)
    low = column(slopes_ref[0:1, :] / PENALTY, rows)
    high = column((slopes_ref[0:1, :] + slopes_ref[1:2, :]) / PENALTY, rows)
    for block in range(blocks):
        span = pl.ds(block * size, size)
        initial = holdings_ref[:, span]
        primal = primal_ref[:, span] if last else initial
        grad = terms[block]
        expected = expected_ref[:, span]
        allowed = eligible_ref[:, span].astype(jnp.float32)
        if last:
            dual = dual_ref[:, span]
            gap = primal - traded_ref[:, span] + dual
        else:
            dual = jnp.zeros_like(initial)
            gap = dual
        primal = allowed * (primal - STEP_SIZE * (RISK_AVERSION * grad - expected + PENALTY * gap))
        shifted = primal + dual - initial
        knee = knee_levels_ref[knee_index_ref[block]]
        magnitude = jnp.abs(shifted)
        moved = jnp.minimum(jnp.maximum(magnitude - low, 0.0), knee) + jnp.maximum(
            magnitude - high - knee, 0.0
        )
        traded = initial + jnp.where(shifted < 0.0, -moved, moved)
        traded_out[:, span] = traded
        dual_out[:, span] = dual + primal - traded
        if not last:
            primal_out[:, span] = primal
            wire_ref[block] = primal.astype(jnp.bfloat16)
    if not last:
        fill_outgoing(served_ref, me_ref, wire_ref, outgoing)


def body(
    holdings,
    eligible,
    returns_mu,
    cov_diag,
    cov_pairs,
    pair_slots,
    need_table,
    break_index,
    break_levels,
    cost_slopes,
):
    rows, assets = holdings.shape
    blocks, size, _ = cov_diag.shape
    owners = lax.axis_size("blk")
    my_index = lax.axis_index("blk")
    capacity = need_table.shape[2]
    slots = owners * capacity
    pairs = cov_pairs.shape[0]
    late = tuple(rank for rank, offset in enumerate(order(owners)) if offset in (owners // 2 + 1, owners // 2))
    early = tuple(rank for rank in range(owners) if rank not in late)
    width = -(-(pairs + LANES) // 128) * 128
    me = my_index.reshape(1)
    served = lax.dynamic_index_in_dim(need_table, my_index, 1, keepdims=False).reshape(-1)
    wire_scratch = pltpu.VMEM((blocks, rows, size), jnp.bfloat16)
    whole = jax.ShapeDtypeStruct((rows, assets), jnp.float32)
    slot_scratch = pltpu.VMEM((slots, rows, size), jnp.bfloat16)
    sent = jax.ShapeDtypeStruct((capacity, rows, size), jnp.bfloat16)
    kept = jax.ShapeDtypeStruct((capacity, rows, size), jnp.float32)

    def cost(count):
        return pl.CostEstimate(
            flops=2 * count * rows * size * size, bytes_accessed=2 * count * size * size, transcendentals=0
        )

    def exchange(values):
        return [values[0]] + [
            lax.ppermute(value, "blk", [(index, index ^ offset) for index in range(owners)])
            for offset, value in zip(order(owners)[1:], values[1:])
        ]

    outgoing = pl.pallas_call(
        pack_kernel,
        out_shape=[sent] * owners,
        in_specs=[SMEM, SMEM, VMEM],
        out_specs=[VMEM] * owners,
        scratch_shapes=[wire_scratch],
        compiler_params=PARAMS,
        cost_estimate=pl.CostEstimate(flops=10**11, bytes_accessed=64 << 20, transcendentals=10**8),
        name="pack_holdings",
    )(served, me, holdings)
    staged, places = pl.pallas_call(
        functools.partial(stage_kernel, owners, capacity),
        out_shape=[
            jax.ShapeDtypeStruct(cov_pairs.shape, cov_pairs.dtype),
            jax.ShapeDtypeStruct((8, -(-pairs // 128) * 128), jnp.int32),
        ],
        in_specs=[HBM, VMEM, SMEM],
        out_specs=[VMEM, VMEM],
        scratch_shapes=[pltpu.SemaphoreType.DMA((4,))],
        compiler_params=pltpu.CompilerParams(vmem_limit_bytes=12 * 1024 * 1024),
        cost_estimate=pl.CostEstimate(flops=0, bytes_accessed=2 * cov_pairs.size, transcendentals=0),
        name="stage_pairs",
    )(cov_pairs, pair_slots, me)
    expected = returns_mu.reshape(1, assets)
    state = ()
    for iteration in range(ITERS):
        last = iteration == ITERS - 1
        incoming = exchange(outgoing)
        if iteration == 0:
            partial_sums = pl.pallas_call(
                functools.partial(pairs_kernel, owners),
                out_shape=[kept] + [sent] * (owners - 1),
                in_specs=[SMEM] + [VMEM] * (1 + owners),
                out_specs=[VMEM] * owners,
                scratch_shapes=[
                    pltpu.VMEM((owners * capacity, rows, size), jnp.bfloat16),
                    pltpu.VMEM((owners * capacity, rows, size), jnp.float32),
                ],
                compiler_params=PARAMS,
                name="pair_products",
            )(places, staged, *incoming)
            plan = pl.pallas_call(
                functools.partial(plan_kernel, owners, capacity, late),
                out_shape=jax.ShapeDtypeStruct((8, width), jnp.int32),
                in_specs=[VMEM, SMEM, ANY],
                out_specs=VMEM,
                compiler_params=PARAMS,
                cost_estimate=pl.CostEstimate(flops=0, bytes_accessed=1 << 20, transcendentals=0),
                name="plan_products",
            )(pair_slots, me, partial_sums[0])
        else:
            total_shape = (slots + 1, rows, size)
            total = pl.pallas_call(
                functools.partial(early_kernel, early),
                out_shape=jax.ShapeDtypeStruct(total_shape, jnp.float32),
                in_specs=[SMEM] + [VMEM] * (1 + len(early)),
                out_specs=VMEM,
                scratch_shapes=[slot_scratch],
                compiler_params=PARAMS,
                cost_estimate=cost(pairs),
                name="early_products",
            )(plan, cov_pairs, *(incoming[rank] for rank in early))
            partial_sums = pl.pallas_call(
                functools.partial(late_kernel, late),
                out_shape=([] if OWN else [kept]) + [sent] * (owners - 1),
                in_specs=[SMEM] + [VMEM] * (2 + len(late)),
                out_specs=[VMEM] * (owners - int(OWN)),
                scratch_shapes=[slot_scratch, pltpu.VMEM(total_shape, jnp.float32)],
                compiler_params=PARAMS,
                cost_estimate=cost(pairs),
                name="late_products",
            )(plan, cov_pairs, total, *(incoming[rank] for rank in late))
            if OWN:
                own = pl.pallas_call(
                    functools.partial(own_kernel, owners),
                    out_shape=kept,
                    in_specs=[SMEM] + [VMEM] * (1 + owners),
                    out_specs=VMEM,
                    scratch_shapes=[slot_scratch, pltpu.VMEM(total_shape, jnp.float32)],
                    compiler_params=PARAMS,
                    cost_estimate=cost(pairs // 2),
                    name="own_products",
                )(plan, cov_pairs, *incoming)
                partial_sums = [own, *partial_sums]
        returned = exchange(partial_sums)
        offsets = order(owners)
        rest = late + tuple(rank for rank in early if offsets[rank] == 1)
        soon = tuple(rank for rank in early if rank not in rest)
        terms = pl.pallas_call(
            functools.partial(terms_kernel, [offsets[rank] for rank in soon]),
            out_shape=jax.ShapeDtypeStruct((blocks, rows, size), jnp.float32),
            in_specs=[SMEM] * 2 + [VMEM] * (2 + len(soon)),
            out_specs=VMEM,
            compiler_params=PARAMS,
            cost_estimate=cost(blocks),
            name="early_terms",
        )(served, me, cov_diag, state[0] if last else holdings, *(returned[rank] for rank in soon))
        outs = pl.pallas_call(
            functools.partial(update_kernel, last, [offsets[rank] for rank in rest]),
            out_shape=[whole] * 2 if last else [whole] * 3 + [sent] * owners,
            in_specs=[SMEM] * 4 + [VMEM] * (5 + len(rest) + len(state)),
            out_specs=[VMEM] * (2 if last else 3 + owners),
            scratch_shapes=[pltpu.VMEM((blocks, rows, size), jnp.float32)] + ([] if last else [wire_scratch]),
            compiler_params=PARAMS,
            name="update",
        )(
            served,
            me,
            break_index,
            break_levels,
            cost_slopes,
            holdings,
            eligible,
            expected,
            terms,
            *(returned[rank] for rank in rest),
            *state,
        )
        if not last:
            state, outgoing = outs[:3], outs[3:]
    return tuple(outs)


def solution(mesh):
    placed = (
        P(("groups", "mand"), "blk"),
        P(("groups", "mand"), "blk"),
        P(("groups", "blk")),
        P(("groups", "blk"), None, None),
        P(("groups", "blk"), None, None),
        P(("groups", "blk"), None, None),
        P("groups", None, None),
        P(("groups", "blk")),
        P(),
        P(None, "mand"),
    )
    return jax.shard_map(
        body,
        mesh=mesh,
        in_specs=placed,
        out_specs=(P(("groups", "mand"), "blk"), P(("groups", "mand"), "blk")),
        check_vma=False,
    )
```

```python
import functools

import jax
import jax.numpy as jnp
from jax import lax
from jax.experimental import pallas as pl
from jax.experimental.pallas import tpu as pltpu
from jax.sharding import PartitionSpec as P

ITERS = 2
LANES = 16
LANES_LEFT = 4
OWN = True
STEP_SIZE = 0.5
RISK_AVERSION = 1.0
PENALTY = 1.0

VMEM = pl.BlockSpec(memory_space=pltpu.VMEM)
SMEM = pl.BlockSpec(memory_space=pltpu.SMEM)
ANY = pl.BlockSpec(memory_space=pl.ANY)
HBM = pl.BlockSpec(memory_space=pltpu.HBM)
PARAMS = pltpu.CompilerParams(vmem_limit_bytes=24 * 1024 * 1024)


def order(owners):
    offsets = list(reversed(range(1, owners)))
    offsets[:2] = reversed(offsets[:2])
    for place, offset in ((1, owners // 2 - 1), (3, owners // 2 - 2)):
        offsets.remove(offset)
        offsets.insert(place, offset)
    return (0, *offsets)


def fill_outgoing(served_ref, me_ref, wire_ref, outgoing):
    capacity = outgoing[0].shape[0]
    for offset, out_ref in zip(order(len(outgoing)), outgoing):
        for column_index in range(capacity):
            local = served_ref[(offset ^ me_ref[0]) * capacity + column_index]
            out_ref[column_index] = wire_ref[jnp.maximum(local, 0)]


def pack_kernel(served_ref, me_ref, holdings_ref, *refs):
    *outgoing, wire_ref = refs
    size = wire_ref.shape[2]
    for block in range(wire_ref.shape[0]):
        wire_ref[block] = holdings_ref[:, block * size : (block + 1) * size].astype(jnp.bfloat16)
    fill_outgoing(served_ref, me_ref, wire_ref, outgoing)


def ranked(slot, me, owners, capacity):
    owner = lax.div(slot, jnp.full_like(slot, capacity))
    rank = jnp.zeros_like(slot)
    for candidate, offset in enumerate(order(owners)):
        rank = jnp.where(owner ^ me == offset, candidate, rank)
    return rank, rank * capacity + slot - owner * capacity


def stage_kernel(owners, capacity, cov_ref, pairs_ref, me_ref, staged_ref, places_ref, sems):
    parts = sems.shape[0]
    step = cov_ref.shape[0] // parts
    copies = [
        pltpu.make_async_copy(
            cov_ref.at[pl.ds(part * step, step)], staged_ref.at[pl.ds(part * step, step)], sems.at[part]
        )
        for part in range(parts)
    ]
    for copy in copies:
        copy.start()
    pairs, width = pairs_ref.shape[1], places_ref.shape[1]
    shape = (pairs, width)
    lane_is_pair = lax.broadcasted_iota(jnp.int32, shape, 0) == lax.broadcasted_iota(jnp.int32, shape, 1)
    places_ref[...] = jnp.zeros_like(places_ref)
    for side in range(2):
        place = ranked(pairs_ref[0, :, side : side + 1], me_ref[0], owners, capacity)[1]
        places_ref[pl.ds(side, 1), :] = jnp.sum(jnp.where(lane_is_pair, place, 0), axis=0, keepdims=True)
    for copy in copies:
        copy.wait()


def pairs_kernel(owners, places_ref, cov_ref, *refs):
    incoming, partial, (slot_rows, total) = refs[:owners], refs[owners : 2 * owners], refs[2 * owners :]
    capacity = incoming[0].shape[0]
    for rank, rows_ref in enumerate(incoming):
        slot_rows[pl.ds(rank * capacity, capacity)] = rows_ref[...]
    total[...] = jnp.zeros_like(total)

    def one(pair, carry):
        first = places_ref[0, pair]
        second = places_ref[1, pair]
        block = cov_ref[pair]
        to_first = lax.dot_general(
            slot_rows[second], block, (((1,), (1,)), ((), ())), preferred_element_type=jnp.float32
        )
        to_second = jnp.dot(slot_rows[first], block, preferred_element_type=jnp.float32)
        total[first] += to_first
        total[second] += to_second
        return carry

    lax.fori_loop(0, cov_ref.shape[0], one, 0, unroll=64)
    for rank, out_ref in enumerate(partial):
        out_ref[...] = total[pl.ds(rank * capacity, capacity)].astype(out_ref.dtype)


def plan_kernel(owners, capacity, late, pairs_ref, me_ref, after_ref, plan_ref):
    pairs, width = pairs_ref.shape[1], plan_ref.shape[1]
    slots = owners * capacity
    bits = slots.bit_length()
    shape = (pairs, width)
    pair = lax.broadcasted_iota(jnp.int32, (pairs, 1), 0)
    lane = lax.broadcasted_iota(jnp.int32, shape, 1)

    (rank0, place0), (rank1, place1) = (
        ranked(pairs_ref[0, :, side : side + 1], me_ref[0], owners, capacity) for side in range(2)
    )
    sides = []
    for side, (rank, source, target) in enumerate(((rank0, place0, place1), (rank1, place1, place0))):
        group = jnp.zeros_like(rank)
        for late_rank in late:
            group = jnp.where(rank == late_rank, 1, group)
        if OWN:
            group = jnp.where(target < capacity, 2, group)
        entry = (((pair << bits) | source) << bits) | target
        sides.append((group, entry, (lane == 2 * group + side).astype(jnp.float32)))
    square = (pairs, pairs)
    before = lax.broadcasted_iota(jnp.int32, square, 1) <= lax.broadcasted_iota(jnp.int32, square, 0)
    counts = jnp.dot(
        before.astype(jnp.bfloat16),
        (sides[0][2] + sides[1][2]).astype(jnp.bfloat16),
        preferred_element_type=jnp.float32,
    )
    for side, (group, entry, member) in enumerate(sides):
        position = jnp.sum(member * counts, axis=1, keepdims=True).astype(jnp.int32) - 1
        for index in range(3):
            listed = (position == lane) & (group == index)
            row = jnp.sum(jnp.where(listed, (entry - slots).astype(jnp.float32), 0.0), axis=0, keepdims=True)
            plan_ref[pl.ds(2 * index + side, 1), :] = row.astype(jnp.int32) + slots
    plan_ref[pl.ds(6, 1), :] = counts[pairs - 1 : pairs, :].astype(jnp.int32)
    plan_ref[pl.ds(7, 1), :] = jnp.zeros((1, width), jnp.int32)


def products(group, plan_ref, cov_ref, slot_rows, total):
    bits = slot_rows.shape[0].bit_length()
    mask = (1 << bits) - 1
    longest = jnp.maximum(plan_ref[6, 2 * group], plan_ref[6, 2 * group + 1])

    def steps(start, lanes):
        def one(step, carry):
            for lane in range(lanes):
                for side in range(2):
                    entry = plan_ref[2 * group + side, start + step * lanes + lane]
                    term = lax.dot_general(
                        slot_rows[(entry >> bits) & mask],
                        cov_ref[entry >> (2 * bits)],
                        (((1,), (side,)), ((), ())),
                        preferred_element_type=jnp.float32,
                    )
                    total[entry & mask] += term
            return carry

        return one

    whole = lax.div(longest, LANES)
    done = whole * LANES
    lax.fori_loop(0, whole, steps(0, LANES), 0)
    lax.fori_loop(0, lax.div(longest - done + LANES_LEFT - 1, LANES_LEFT), steps(done, LANES_LEFT), 0)


def gather_rows(ranks, incoming, slot_rows):
    capacity = incoming[0].shape[0]
    for rank, rows_ref in zip(ranks, incoming):
        slot_rows[pl.ds(rank * capacity, capacity)] = rows_ref[...]


def early_kernel(ranks, plan_ref, cov_ref, *refs):
    *incoming, total, slot_rows = refs
    gather_rows(ranks, incoming, slot_rows)
    total[...] = jnp.zeros_like(total)
    products(0, plan_ref, cov_ref, slot_rows, total)


def late_kernel(ranks, plan_ref, cov_ref, early_ref, *refs):
    incoming, outs, (slot_rows, total) = refs[: len(ranks)], refs[len(ranks) : -2], refs[-2:]
    capacity = incoming[0].shape[0]
    gather_rows(ranks, incoming, slot_rows)
    total[...] = early_ref[...]
    products(1, plan_ref, cov_ref, slot_rows, total)
    for rank, out_ref in enumerate(outs, int(OWN)):
        out_ref[...] = total[pl.ds(rank * capacity, capacity)].astype(out_ref.dtype)


def own_kernel(owners, plan_ref, cov_ref, *refs):
    incoming, (out_ref, slot_rows, total) = refs[:owners], refs[owners:]
    capacity = incoming[0].shape[0]
    gather_rows(range(owners), incoming, slot_rows)
    total[pl.ds(0, capacity)] = jnp.zeros(out_ref.shape, jnp.float32)
    products(2, plan_ref, cov_ref, slot_rows, total)
    out_ref[...] = total[pl.ds(0, capacity)]


def column(row, rows):
    square = (rows, rows)
    on_diagonal = lax.broadcasted_iota(jnp.int32, square, 0) == lax.broadcasted_iota(jnp.int32, square, 1)
    return jnp.sum(jnp.where(on_diagonal, row, 0.0), axis=1, keepdims=True)


def add_returned(served_ref, me_ref, offsets, returned, terms):
    capacity = returned[0].shape[0]
    for offset, back_ref in zip(offsets, returned):
        for column_index in range(capacity):
            local = served_ref[(offset ^ me_ref[0]) * capacity + column_index]

            @pl.when(local >= 0)
            def _(local=local, back_ref=back_ref, column_index=column_index):
                terms[local] += back_ref[column_index].astype(jnp.float32)


def terms_kernel(offsets, served_ref, me_ref, diag_ref, primal_ref, *refs):
    *returned, terms = refs
    blocks, _, size = terms.shape
    for block in range(blocks):
        x_wire = primal_ref[:, block * size : (block + 1) * size].astype(jnp.bfloat16)
        terms[block] = jnp.dot(x_wire, diag_ref[block], preferred_element_type=jnp.float32)
    add_returned(served_ref, me_ref, offsets, returned, terms)


def update_kernel(
    last,
    offsets,
    served_ref,
    me_ref,
    knee_index_ref,
    knee_levels_ref,
    slopes_ref,
    holdings_ref,
    eligible_ref,
    expected_ref,
    terms_ref,
    *refs,
):
    returned, refs = refs[: len(offsets)], refs[len(offsets) :]
    if last:
        primal_ref, traded_ref, dual_ref, traded_out, dual_out, terms = refs
    else:
        primal_out, traded_out, dual_out, *outgoing, terms, wire_ref = refs
    blocks, rows, size = terms.shape
    terms[...] = terms_ref[...]
    add_returned(served_ref, me_ref, offsets, returned, terms)
    low = column(slopes_ref[0:1, :] / PENALTY, rows)
    high = column((slopes_ref[0:1, :] + slopes_ref[1:2, :]) / PENALTY, rows)
    for block in range(blocks):
        span = pl.ds(block * size, size)
        initial = holdings_ref[:, span]
        primal = primal_ref[:, span] if last else initial
        grad = terms[block]
        expected = expected_ref[:, span]
        allowed = eligible_ref[:, span].astype(jnp.float32)
        if last:
            dual = dual_ref[:, span]
            gap = primal - traded_ref[:, span] + dual
        else:
            dual = jnp.zeros_like(initial)
            gap = dual
        primal = allowed * (primal - STEP_SIZE * (RISK_AVERSION * grad - expected + PENALTY * gap))
        shifted = primal + dual - initial
        knee = knee_levels_ref[knee_index_ref[block]]
        magnitude = jnp.abs(shifted)
        moved = jnp.minimum(jnp.maximum(magnitude - low, 0.0), knee) + jnp.maximum(
            magnitude - high - knee, 0.0
        )
        traded = initial + jnp.where(shifted < 0.0, -moved, moved)
        traded_out[:, span] = traded
        dual_out[:, span] = dual + primal - traded
        if not last:
            primal_out[:, span] = primal
            wire_ref[block] = primal.astype(jnp.bfloat16)
    if not last:
        fill_outgoing(served_ref, me_ref, wire_ref, outgoing)


def body(
    holdings,
    eligible,
    returns_mu,
    cov_diag,
    cov_pairs,
    pair_slots,
    need_table,
    break_index,
    break_levels,
    cost_slopes,
):
    rows, assets = holdings.shape
    blocks, size, _ = cov_diag.shape
    owners = lax.axis_size("blk")
    my_index = lax.axis_index("blk")
    capacity = need_table.shape[2]
    slots = owners * capacity
    pairs = cov_pairs.shape[0]
    late = tuple(rank for rank, offset in enumerate(order(owners)) if offset in (owners // 2 + 1, owners // 2))
    early = tuple(rank for rank in range(owners) if rank not in late)
    width = -(-(pairs + LANES) // 128) * 128
    me = my_index.reshape(1)
    served = lax.dynamic_index_in_dim(need_table, my_index, 1, keepdims=False).reshape(-1)
    wire_scratch = pltpu.VMEM((blocks, rows, size), jnp.bfloat16)
    whole = jax.ShapeDtypeStruct((rows, assets), jnp.float32)
    slot_scratch = pltpu.VMEM((slots, rows, size), jnp.bfloat16)
    sent = jax.ShapeDtypeStruct((capacity, rows, size), jnp.bfloat16)
    kept = jax.ShapeDtypeStruct((capacity, rows, size), jnp.float32)

    def cost(count):
        return pl.CostEstimate(
            flops=2 * count * rows * size * size, bytes_accessed=2 * count * size * size, transcendentals=0
        )

    def exchange(values):
        return [values[0]] + [
            lax.ppermute(value, "blk", [(index, index ^ offset) for index in range(owners)])
            for offset, value in zip(order(owners)[1:], values[1:])
        ]

    outgoing = pl.pallas_call(
        pack_kernel,
        out_shape=[sent] * owners,
        in_specs=[SMEM, SMEM, VMEM],
        out_specs=[VMEM] * owners,
        scratch_shapes=[wire_scratch],
        compiler_params=PARAMS,
        cost_estimate=pl.CostEstimate(flops=10**11, bytes_accessed=64 << 20, transcendentals=10**8),
        name="pack_holdings",
    )(served, me, holdings)
    staged, places = pl.pallas_call(
        functools.partial(stage_kernel, owners, capacity),
        out_shape=[
            jax.ShapeDtypeStruct(cov_pairs.shape, cov_pairs.dtype),
            jax.ShapeDtypeStruct((8, -(-pairs // 128) * 128), jnp.int32),
        ],
        in_specs=[HBM, VMEM, SMEM],
        out_specs=[VMEM, VMEM],
        scratch_shapes=[pltpu.SemaphoreType.DMA((4,))],
        compiler_params=pltpu.CompilerParams(vmem_limit_bytes=12 * 1024 * 1024),
        cost_estimate=pl.CostEstimate(flops=0, bytes_accessed=2 * cov_pairs.size, transcendentals=0),
        name="stage_pairs",
    )(cov_pairs, pair_slots, me)
    expected = returns_mu.reshape(1, assets)
    state = ()
    for iteration in range(ITERS):
        last = iteration == ITERS - 1
        incoming = exchange(outgoing)
        if iteration == 0:
            partial_sums = pl.pallas_call(
                functools.partial(pairs_kernel, owners),
                out_shape=[kept] + [sent] * (owners - 1),
                in_specs=[SMEM] + [VMEM] * (1 + owners),
                out_specs=[VMEM] * owners,
                scratch_shapes=[
                    pltpu.VMEM((owners * capacity, rows, size), jnp.bfloat16),
                    pltpu.VMEM((owners * capacity, rows, size), jnp.float32),
                ],
                compiler_params=PARAMS,
                name="pair_products",
            )(places, staged, *incoming)
            plan = pl.pallas_call(
                functools.partial(plan_kernel, owners, capacity, late),
                out_shape=jax.ShapeDtypeStruct((8, width), jnp.int32),
                in_specs=[VMEM, SMEM, ANY],
                out_specs=VMEM,
                compiler_params=PARAMS,
                cost_estimate=pl.CostEstimate(flops=0, bytes_accessed=1 << 20, transcendentals=0),
                name="plan_products",
            )(pair_slots, me, partial_sums[0])
        else:
            total_shape = (slots + 1, rows, size)
            total = pl.pallas_call(
                functools.partial(early_kernel, early),
                out_shape=jax.ShapeDtypeStruct(total_shape, jnp.float32),
                in_specs=[SMEM] + [VMEM] * (1 + len(early)),
                out_specs=VMEM,
                scratch_shapes=[slot_scratch],
                compiler_params=PARAMS,
                cost_estimate=cost(pairs),
                name="early_products",
            )(plan, cov_pairs, *(incoming[rank] for rank in early))
            partial_sums = pl.pallas_call(
                functools.partial(late_kernel, late),
                out_shape=([] if OWN else [kept]) + [sent] * (owners - 1),
                in_specs=[SMEM] + [VMEM] * (2 + len(late)),
                out_specs=[VMEM] * (owners - int(OWN)),
                scratch_shapes=[slot_scratch, pltpu.VMEM(total_shape, jnp.float32)],
                compiler_params=PARAMS,
                cost_estimate=cost(pairs),
                name="late_products",
            )(plan, cov_pairs, total, *(incoming[rank] for rank in late))
            if OWN:
                own = pl.pallas_call(
                    functools.partial(own_kernel, owners),
                    out_shape=kept,
                    in_specs=[SMEM] + [VMEM] * (1 + owners),
                    out_specs=VMEM,
                    scratch_shapes=[slot_scratch, pltpu.VMEM(total_shape, jnp.float32)],
                    compiler_params=PARAMS,
                    cost_estimate=cost(pairs // 2),
                    name="own_products",
                )(plan, cov_pairs, *incoming)
                partial_sums = [own, *partial_sums]
        returned = exchange(partial_sums)
        offsets = order(owners)
        rest = late + tuple(rank for rank in early if offsets[rank] == 1)
        soon = tuple(rank for rank in early if rank not in rest)
        terms = pl.pallas_call(
            functools.partial(terms_kernel, [offsets[rank] for rank in soon]),
            out_shape=jax.ShapeDtypeStruct((blocks, rows, size), jnp.float32),
            in_specs=[SMEM] * 2 + [VMEM] * (2 + len(soon)),
            out_specs=VMEM,
            compiler_params=PARAMS,
            cost_estimate=cost(blocks),
            name="early_terms",
        )(served, me, cov_diag, state[0] if last else holdings, *(returned[rank] for rank in soon))
        outs = pl.pallas_call(
            functools.partial(update_kernel, last, [offsets[rank] for rank in rest]),
            out_shape=[whole] * 2 if last else [whole] * 3 + [sent] * owners,
            in_specs=[SMEM] * 4 + [VMEM] * (5 + len(rest) + len(state)),
            out_specs=[VMEM] * (2 if last else 3 + owners),
            scratch_shapes=[pltpu.VMEM((blocks, rows, size), jnp.float32)] + ([] if last else [wire_scratch]),
            compiler_params=PARAMS,
            name="update",
        )(
            served,
            me,
            break_index,
            break_levels,
            cost_slopes,
            holdings,
            eligible,
            expected,
            terms,
            *(returned[rank] for rank in rest),
            *state,
        )
        if not last:
            state, outgoing = outs[:3], outs[3:]
    return tuple(outs)


def solution(mesh):
    placed = (
        P(("groups", "mand"), "blk"),
        P(("groups", "mand"), "blk"),
        P(("groups", "blk")),
        P(("groups", "blk"), None, None),
        P(("groups", "blk"), None, None),
        P(("groups", "blk"), None, None),
        P("groups", None, None),
        P(("groups", "blk")),
        P(),
        P(None, "mand"),
    )
    return jax.shard_map(
        body,
        mesh=mesh,
        in_specs=placed,
        out_specs=(P(("groups", "mand"), "blk"), P(("groups", "mand"), "blk")),
        check_vma=False,
    )
```
